128 devices in a mesh: lat: 8 (over y, core), lon: 16 (over x, z).
Axes of the slice: x: 4, y: 4, z: 4, core: 2. Of those that a mesh axis runs over, the one named last changes fastest.
Arguments:
- grid_nodes: bfloat16 [128, 1024, 512], P('lat', 'lon'), may hold values from -6 to 6
- mesh_nodes: bfloat16 [65536, 512], P(('lat', 'lon')), may hold values from -6 to 6
- g2m_edges: bfloat16 [1792, 128, 512], P(('lat', 'lon')), may hold values from -6 to 6
- mesh_edges: bfloat16 [2048, 128, 512], P(('lat', 'lon')), may hold values from -6 to 6
- g2m_sender: int32 [1792, 128], P(('lat', 'lon')), may hold values from 0 to 1727, as said below
- g2m_receiver: int32 [1792, 128], P(('lat', 'lon')), may hold values from -1 to 127, as said below
- g2m_window: int32 [1792], P(('lat', 'lon')), may hold values from 0 to 3, as said below
- mesh_sender: int32 [2048, 128], P(('lat', 'lon')), may hold values from 0 to 4287, as said below
- mesh_receiver: int32 [2048, 128], P(('lat', 'lon')), may hold values from -1 to 127, as said below
- mesh_window: int32 [2048], P(('lat', 'lon')), may hold values from 0 to 3, as said below
- near_rows: int32 [128, 9, 192], P(('lat', 'lon')), may hold values from -1 to 511, as said below
- far_rows: int32 [128, 128, 16], P(('lat', 'lon')), may hold values from -1 to 511, as said below
- w_g2m_edge: bfloat16 [4, 512, 512], replicated, may hold values from -0.25 to 0.25
- w_mesh_node: bfloat16 [3, 512, 512], replicated, may hold values from -0.25 to 0.25
- w_grid_node: bfloat16 [2, 512, 512], replicated, may hold values from -0.25 to 0.25
- w_proc_edge: bfloat16 [4, 512, 512], replicated, may hold values from -0.25 to 0.25
- w_proc_node: bfloat16 [3, 512, 512], replicated, may hold values from -0.25 to 0.25
- norms: float32 [5, 2, 512], replicated, may hold values from 0.1 to 1.9
Outputs:
- mesh_out: bfloat16 [65536, 512], P(('lat', 'lon'))
- grid_out: bfloat16 [128, 1024, 512], P('lat', 'lon')
The draws below stay inside these ranges and needn't reach their ends.
Inputs may be any that keep to these rules, and one draw needn't show every extreme that they name: `g2m_sender`: flat index i * 72 + j of a cell of the owning device's grid block extended by 4 cells on every side; no edge names a cell above the first or below the last grid row. `g2m_receiver`: position of the receiving mesh node in the block's window of 128 of the device's mesh nodes; -1 marks an empty slot. `g2m_window`: window of 128 of the device's own mesh nodes that holds the block's receivers. `mesh_sender`: below 512: one of the device's own mesh nodes. From 512 to 2239: slot s of the list that the neighbouring patch at relative position q sends to this device, and that patch exists and the slot is live. Above: slot s of the list that device p sends to this device, and that slot is live. Every device's edges read the first slot of every other device's list to it. `mesh_receiver`: position of the receiving mesh node in the block's window of 128 of the device's mesh nodes; -1 marks an empty slot. `mesh_window`: window of 128 of the device's own mesh nodes that holds the block's receivers. `near_rows`: entry [p, q] lists own mesh nodes of device p sent to the patch at band offset q // 3 - 1 and sector offset q % 3 - 1 (sectors periodic): between 64 and 192 live entries first, then -1. Entry q = 4 and entries towards bands that don't exist hold only -1. Every device fills all 192 slots of its list to one of its two sector neighbours. `far_rows`: entry [p, q] lists own mesh nodes of device p sent to device q: between 5 and 16 live entries first, then -1. A device sends nothing to itself, and every device fills all 16 slots of its list to some other device.
All inputs are finite; a program needn't handle non-finite values.
Results may differ from the reference program's by a relative error of at most 0.006.
Values may be sent and summed in bfloat16 or wider, within the bound.
A program may use at most 128 MiB of HBM per device.

```python
import jax
import jax.numpy as jnp
from jax import lax

D = 512
GR = 16
GC = 64
HW = 4
M_DEV = 512
ENCODER_GROUPS = 14
LINK_GROUPS = 16
NCAP = 192
FAR = 16
NGR = 128
NGC = 1024
MESH_NODES = 65536
G2M_BLOCKS = 1792
MESH_BLOCKS = 2048
N_LAT = 8
N_LON = 16


def traffic(key):
    chip_quantity = N_LAT * N_LON
    key_one, key_two, key_three, key_four, random_key_fifth, random_key_sixth = jax.random.split(key, 6)
    device_ids = jnp.arange(chip_quantity, dtype=jnp.int32)
    band_index = device_ids // N_LON
    codes = jnp.arange(9, dtype=jnp.int32)
    lat_step = codes // 3 - 1
    target_band = band_index[:, None] + lat_step[None, :]
    valid = (target_band >= 0) & (target_band < N_LAT) & (codes != 4)[None, :]
    near_counts = jax.random.randint(key_one, (chip_quantity, 9), NCAP // 3, NCAP + 1)
    full_pick = 3 + 2 * jax.random.randint(key_two, (chip_quantity,), 0, 2)
    near_counts = jnp.where(codes[None, :] == full_pick[:, None], NCAP, near_counts)
    near_counts = jnp.where(valid, near_counts, 0)
    near_nodes = jax.random.randint(key_three, (chip_quantity, 9, NCAP), 0, M_DEV)
    near_nodes = near_nodes.at[0, 5, 0].set(M_DEV - 1)
    near_slots = jnp.arange(NCAP, dtype=jnp.int32)
    near_nodes = jnp.where(near_slots[None, None, :] < near_counts[:, :, None], near_nodes, -1)
    far_counts = jax.random.randint(key_four, (chip_quantity, chip_quantity), FAR // 3, FAR + 1)
    shifts = jax.random.randint(random_key_fifth, (chip_quantity,), 1, chip_quantity)
    full_to = (device_ids + shifts) % chip_quantity
    far_counts = jnp.where(device_ids[None, :] == full_to[:, None], FAR, far_counts)
    far_counts = far_counts.at[chip_quantity - 1, 0].set(FAR)
    far_counts = jnp.where(device_ids[:, None] == device_ids[None, :], 0, far_counts)
    far_nodes = jax.random.randint(random_key_sixth, (chip_quantity, chip_quantity, FAR), 0, M_DEV)
    far_nodes = far_nodes.at[chip_quantity - 1, 0, FAR - 1].set(M_DEV - 1)
    far_slots = jnp.arange(FAR, dtype=jnp.int32)
    far_nodes = jnp.where(far_slots[None, None, :] < far_counts[:, :, None], far_nodes, -1)
    return (near_counts, near_nodes, far_counts, far_nodes)


def draw_near_rows(key, part):
    near_counts, near_nodes, far_counts, far_nodes = traffic(key)
    return near_nodes


def draw_far_rows(key, part):
    near_counts, near_nodes, far_counts, far_nodes = traffic(key)
    return far_nodes


def draw_mesh_sender(key, part):
    near_counts, near_nodes, far_counts, far_nodes = traffic(key)
    key = jax.random.fold_in(key, 5)
    chip_quantity = N_LAT * N_LON
    key_one, key_two, key_three, key_four, random_key_fifth = jax.random.split(key, 5)
    edge_dimensions = (chip_quantity, LINK_GROUPS * 128)
    local_pick = jax.random.randint(key_one, edge_dimensions, 0, M_DEV)
    kind_draw = jax.random.randint(key_two, edge_dimensions, 0, 50)
    code_draw = jax.random.randint(key_three, edge_dimensions, 0, 8)
    near_code = code_draw + (code_draw >= 4).astype(jnp.int32)
    device_ids = jnp.arange(chip_quantity, dtype=jnp.int32)[:, None]
    band_index = device_ids // N_LON
    sector = device_ids % N_LON
    target_band = band_index + near_code // 3 - 1
    band_fine = (target_band >= 0) & (target_band < N_LAT)
    near_peer = jnp.clip(target_band, 0, N_LAT - 1) * N_LON + (sector + near_code % 3 - 1) % N_LON
    near_avail = near_counts[near_peer, 8 - near_code]
    slot_draw = jax.random.randint(key_four, edge_dimensions, 0, 1 << 20)
    near_slot = slot_draw % jnp.maximum(near_avail, 1)
    use_near = (kind_draw >= 40) & (kind_draw < 47) & band_fine & (near_avail > 0)
    far_peer = jax.random.randint(random_key_fifth, edge_dimensions, 0, chip_quantity)
    far_avail = far_counts[far_peer, device_ids]
    far_slot = slot_draw % jnp.maximum(far_avail, 1)
    use_far = (kind_draw >= 47) & (far_avail > 0)
    far_code = M_DEV + 9 * NCAP + far_peer * FAR + far_slot
    sender = jnp.where(use_near, M_DEV + near_code * NCAP + near_slot, jnp.where(use_far, far_code, local_pick))
    peer_steps = jnp.arange(1, chip_quantity, dtype=jnp.int32)[None, :]
    every_peer = (device_ids + peer_steps) % chip_quantity
    cover_codes = M_DEV + 9 * NCAP + every_peer * FAR
    sender = sender.at[:, 2:chip_quantity + 1].set(cover_codes)
    sender = sender.at[0, 0].set(M_DEV + 9 * NCAP + (chip_quantity - 1) * FAR + FAR - 1)
    sender = sender.at[0, 1].set(0)
    return sender.reshape(chip_quantity * LINK_GROUPS, 128)


def draw_g2m_sender(key, part):
    key = jax.random.fold_in(key, 1)
    chip_quantity = N_LAT * N_LON
    halo_rows = GR + 2 * HW
    halo_cols = GC + 2 * HW
    key_row, key_col = jax.random.split(key)
    band_index = (jnp.arange(chip_quantity, dtype=jnp.int32) // N_LON)[:, None]
    lowest = jnp.where(band_index == 0, HW, 0)
    highest = jnp.where(band_index == N_LAT - 1, halo_rows - HW, halo_rows)
    row_draw = jax.random.randint(key_row, (chip_quantity, ENCODER_GROUPS * 128), 0, 1 << 20)
    row_index = lowest + row_draw % (highest - lowest)
    col_index = jax.random.randint(key_col, (chip_quantity, ENCODER_GROUPS * 128), 0, halo_cols)
    flat = row_index * halo_cols + col_index
    flat = flat.at[0, 0].set(halo_rows * halo_cols - 1).at[chip_quantity - 1, 0].set(0)
    return flat.reshape(chip_quantity * ENCODER_GROUPS, 128)


def draw_g2m_receiver(key, part):
    key = jax.random.fold_in(key, 2)
    chip_quantity = N_LAT * N_LON
    key_pos, active_seed = jax.random.split(key)
    coordinate_spots = jax.random.randint(key_pos, (chip_quantity, ENCODER_GROUPS, 128), 0, 128)
    band_index = jnp.arange(chip_quantity, dtype=jnp.int32) // N_LON
    thousandth_fraction = 400 + 600 * jnp.abs(2 * band_index - (N_LAT - 1)) // (N_LAT - 1)
    activity_draws = jax.random.randint(active_seed, (chip_quantity, ENCODER_GROUPS, 128), 0, 1000)
    coordinate_spots = jnp.where(activity_draws < thousandth_fraction[:, None, None], coordinate_spots, -1)
    coordinate_spots = coordinate_spots.at[:, 0, 0].set(-1).at[:, 0, 1].set(127)
    return coordinate_spots.reshape(chip_quantity * ENCODER_GROUPS, 128)


def draw_g2m_window(key, part):
    key = jax.random.fold_in(key, 3)
    chip_quantity = N_LAT * N_LON
    windows = jax.random.randint(key, (chip_quantity * ENCODER_GROUPS,), 0, M_DEV // 128)
    return windows.at[0].set(0).at[1].set(M_DEV // 128 - 1)


def draw_mesh_receiver(key, part):
    key = jax.random.fold_in(key, 4)
    chip_quantity = N_LAT * N_LON
    key_pos, active_seed = jax.random.split(key)
    coordinate_spots = jax.random.randint(key_pos, (chip_quantity, LINK_GROUPS, 128), 0, 128)
    activity_draws = jax.random.randint(active_seed, (chip_quantity, LINK_GROUPS, 128), 0, 10)
    coordinate_spots = jnp.where(activity_draws > 0, coordinate_spots, -1)
    coordinate_spots = coordinate_spots.at[:, 0, 0].set(-1).at[:, 0, 1].set(127)
    return coordinate_spots.reshape(chip_quantity * LINK_GROUPS, 128)


def draw_mesh_window(key, part):
    key = jax.random.fold_in(key, 6)
    chip_quantity = N_LAT * N_LON
    windows = jax.random.randint(key, (chip_quantity * LINK_GROUPS,), 0, M_DEV // 128)
    return windows.at[0].set(0).at[1].set(M_DEV // 128 - 1)


def steps_of(rng, extent, pieces, low, high):
    def one(position, parts):
        steps = jax.random.uniform(jax.random.fold_in(jax.random.fold_in(rng, 6), position), (parts,), jnp.float32, low / len(pieces), high / len(pieces))
        return jnp.repeat(jnp.exp(steps), extent[position] // parts).reshape((-1,) + (1,) * (len(extent) - position - 1))

    loudness = one(*pieces[0])
    for cut in pieces[1:]:
        loudness = loudness * one(*cut)
    return loudness


def bell_draw(rng, dims, scale, reach, pieces=(), kind=jnp.bfloat16):
    factor_of = steps_of(rng, dims, pieces, -0.22, 0.18) if pieces else 1.0
    entries = jax.random.normal(rng, dims, jnp.float32) * scale * factor_of
    return jnp.minimum(jnp.maximum(entries, -reach), reach).astype(kind)


def setup_inputs(seed: int = 0) -> dict:
    keys = jax.random.split(jax.random.key(seed), 19)
    grid_nodes = bell_draw(keys[0], (NGR, NGC, D), 1.0, 6.0, ((0, 8), (1, 16)))
    mesh_nodes = bell_draw(keys[1], (MESH_NODES, D), 1.0, 6.0, ((0, 128),))
    g2m_edges = bell_draw(keys[2], (G2M_BLOCKS, 128, D), 1.0, 6.0, ((0, 128),))
    mesh_edges = bell_draw(keys[3], (MESH_BLOCKS, 128, D), 1.0, 6.0, ((0, 128),))
    g2m_sender = draw_g2m_sender(jax.random.fold_in(keys[18], 71), 0)
    g2m_receiver = draw_g2m_receiver(jax.random.fold_in(keys[18], 71), 0)
    g2m_window = draw_g2m_window(jax.random.fold_in(keys[18], 71), 0)
    mesh_sender = draw_mesh_sender(jax.random.fold_in(keys[18], 71), 0)
    mesh_receiver = draw_mesh_receiver(jax.random.fold_in(keys[18], 71), 0)
    mesh_window = draw_mesh_window(jax.random.fold_in(keys[18], 71), 0)
    near_rows = draw_near_rows(jax.random.fold_in(keys[18], 71), 0)
    far_rows = draw_far_rows(jax.random.fold_in(keys[18], 71), 0)
    w_g2m_edge = bell_draw(keys[12], (4, D, D), D ** -0.5, 0.25)
    w_mesh_node = bell_draw(keys[13], (3, D, D), D ** -0.5, 0.25)
    w_grid_node = bell_draw(keys[14], (2, D, D), D ** -0.5, 0.25)
    w_proc_edge = bell_draw(keys[15], (4, D, D), D ** -0.5, 0.25)
    w_proc_node = bell_draw(keys[16], (3, D, D), D ** -0.5, 0.25)
    norms = jnp.clip(1.0 + 0.18 * jax.random.normal(keys[17], (5, 2, D), jnp.float32), 0.1, 1.9)
    return {"grid_nodes": grid_nodes, "mesh_nodes": mesh_nodes, "g2m_edges": g2m_edges, "mesh_edges": mesh_edges, "g2m_sender": g2m_sender, "g2m_receiver": g2m_receiver, "g2m_window": g2m_window, "mesh_sender": mesh_sender, "mesh_receiver": mesh_receiver, "mesh_window": mesh_window, "near_rows": near_rows, "far_rows": far_rows, "w_g2m_edge": w_g2m_edge, "w_mesh_node": w_mesh_node, "w_grid_node": w_grid_node, "w_proc_edge": w_proc_edge, "w_proc_node": w_proc_node, "norms": norms}


EPS = 1e-05

def layer_norm(values, norm_pair):
    row_mean = lax.optimization_barrier(jnp.mean(values, axis=-1, keepdims=True))
    centred = values - row_mean
    variance = lax.optimization_barrier(jnp.mean(centred * centred, axis=-1, keepdims=True))
    return centred * lax.rsqrt(variance + EPS) * norm_pair[0] + norm_pair[1]

def project(node_rows, weight):
    return jnp.dot(node_rows, weight, preferred_element_type=jnp.float32)

def finish(pre_act, w_out, norm_pair):
    hidden = jax.nn.silu(pre_act).astype(jnp.bfloat16)
    return layer_norm(project(hidden, w_out), norm_pair)

def residual_add(base, branch):
    return (base.astype(jnp.float32) + branch).astype(jnp.bfloat16)

def local_rows(receiver, window):
    return (window[:, None] * 128 + jnp.maximum(receiver, 0)).reshape(-1).astype(jnp.int32)

def edge_sum(updated, receiver, window):
    live_edge = (receiver >= 0).reshape(-1)
    row_index = jnp.where(live_edge, local_rows(receiver, window), M_DEV).astype(jnp.int32)
    message_total = jax.ops.segment_sum(updated.astype(jnp.float32), row_index, num_segments=M_DEV + 1)
    return message_total[:M_DEV].astype(jnp.bfloat16)

def reference(grid_nodes, mesh_nodes, g2m_edges, mesh_edges, g2m_sender, g2m_receiver, g2m_window, mesh_sender, mesh_receiver, mesh_window, near_rows, far_rows, w_g2m_edge, w_mesh_node, w_grid_node, w_proc_edge, w_proc_node, norms):
    chip_quantity = N_LAT * N_LON
    halo_cols = GC + 2 * HW
    grid_cols = GC * N_LON
    latent_width = grid_nodes.shape[-1]

    def encode_device(device):
        band_index = device // N_LON
        sector = device % N_LON
        sender = lax.dynamic_slice_in_dim(g2m_sender, device * ENCODER_GROUPS, ENCODER_GROUPS, 0).reshape(-1)
        receiver = lax.dynamic_slice_in_dim(g2m_receiver, device * ENCODER_GROUPS, ENCODER_GROUPS, 0)
        window = lax.dynamic_slice_in_dim(g2m_window, device * ENCODER_GROUPS, ENCODER_GROUPS, 0)
        edges = lax.dynamic_slice_in_dim(g2m_edges, device * ENCODER_GROUPS, ENCODER_GROUPS, 0).reshape(-1, latent_width)
        own_rows = lax.dynamic_slice_in_dim(mesh_nodes, device * M_DEV, M_DEV, 0)
        row_index = (band_index * GR + sender // halo_cols - HW).astype(jnp.int32)
        col_index = ((sector * GC + sender % halo_cols - HW) % grid_cols).astype(jnp.int32)
        sources = grid_nodes[row_index, col_index]
        targets = own_rows[local_rows(receiver, window)]
        pre_act = project(edges, w_g2m_edge[0]) + project(sources, w_g2m_edge[1]) + project(targets, w_g2m_edge[2])
        updated = residual_add(edges, finish(pre_act, w_g2m_edge[3], norms[0]))
        return edge_sum(updated, receiver, window)
    mesh_sum = lax.map(encode_device, jnp.arange(chip_quantity, dtype=jnp.int32)).reshape(-1, latent_width)
    node_pre = project(mesh_nodes, w_mesh_node[0]) + project(mesh_sum, w_mesh_node[1])
    mesh_mid = residual_add(mesh_nodes, finish(node_pre, w_mesh_node[2], norms[1]))

    def grid_block(node_rows):
        return residual_add(node_rows, finish(project(node_rows, w_grid_node[0]), w_grid_node[1], norms[2]))
    grid_out = lax.map(grid_block, grid_nodes.reshape(chip_quantity, -1, latent_width)).reshape(grid_nodes.shape)

    def process_device(device):
        band_index = device // N_LON
        sector = device % N_LON
        sender = lax.dynamic_slice_in_dim(mesh_sender, device * LINK_GROUPS, LINK_GROUPS, 0).reshape(-1)
        receiver = lax.dynamic_slice_in_dim(mesh_receiver, device * LINK_GROUPS, LINK_GROUPS, 0)
        window = lax.dynamic_slice_in_dim(mesh_window, device * LINK_GROUPS, LINK_GROUPS, 0)
        edges = lax.dynamic_slice_in_dim(mesh_edges, device * LINK_GROUPS, LINK_GROUPS, 0).reshape(-1, latent_width)
        displacement_label = sender - M_DEV
        near_code = jnp.clip(displacement_label, 0, 9 * NCAP - 1)
        near_pos = (near_code // NCAP).astype(jnp.int32)
        near_slot = (near_code % NCAP).astype(jnp.int32)
        near_band = jnp.clip(band_index + near_pos // 3 - 1, 0, N_LAT - 1)
        near_peer = (near_band * N_LON + (sector + near_pos % 3 - 1) % N_LON).astype(jnp.int32)
        near_row = jnp.maximum(near_rows[near_peer, 8 - near_pos, near_slot], 0)
        far_code = jnp.maximum(displacement_label - 9 * NCAP, 0)
        far_peer = (far_code // FAR).astype(jnp.int32)
        far_slot = (far_code % FAR).astype(jnp.int32)
        far_row = jnp.maximum(far_rows[far_peer, device, far_slot], 0)
        remote_index = jnp.where(sender < M_DEV + 9 * NCAP, near_peer * M_DEV + near_row, far_peer * M_DEV + far_row)
        row_index = jnp.where(sender < M_DEV, device * M_DEV + sender, remote_index).astype(jnp.int32)
        sources = mesh_mid[row_index]
        own_rows = lax.dynamic_slice_in_dim(mesh_mid, device * M_DEV, M_DEV, 0)
        targets = own_rows[local_rows(receiver, window)]
        pre_act = project(edges, w_proc_edge[0]) + project(sources, w_proc_edge[1]) + project(targets, w_proc_edge[2])
        updated = residual_add(edges, finish(pre_act, w_proc_edge[3], norms[3]))
        return edge_sum(updated, receiver, window)
    proc_sum = lax.map(process_device, jnp.arange(chip_quantity, dtype=jnp.int32)).reshape(-1, latent_width)
    out_pre = project(mesh_mid, w_proc_node[0]) + project(proc_sum, w_proc_node[1])
    mesh_out = residual_add(mesh_mid, finish(out_pre, w_proc_node[2], norms[4]))
    return (mesh_out, grid_out)
```

```python
import jax
import jax.numpy as jnp
from jax import lax
from jax.experimental import pallas as pl
from jax.experimental.pallas import tpu as pltpu
from jax.sharding import PartitionSpec as P

HW = 4
EPS = 1e-05
D = 512
BF16 = jnp.bfloat16
F32 = jnp.float32
MESH = pl.DeviceIdType.MESH

GRID = 1024
HALO = 704
HALO_PAD = 768
NODES = 512
NCAP = 192
NEAR = 9 * NCAP
NEAR_PAD = 1792
FAR = 16
DEVICES = 128
G_EDGES = 1792
P_EDGES = 2048
STEP = 256

G_POS, G_ROW, P_POS, P_ROW, NEAR_IDX, FAR_IDX = 0, 14, 28, 44, 60, 74

FAR_MUL = 77
FAR_INV = 5
FAR_GROUPS = 4
ROUNDS = 7

SEGMENTS = (
    (1, 0, 0, 256),
    (-1, 0, 256, 256),
    (0, 1, 512, 64),
    (0, -1, 576, 64),
    (1, 1, 640, 16),
    (1, -1, 656, 16),
    (-1, 1, 672, 16),
    (-1, -1, 688, 16),
)


def dot(a, b):
    return jnp.dot(a, b, preferred_element_type=F32)


def silu(v):
    half = 0.5 * v
    return (half + half * jnp.tanh(half)).astype(BF16)


def layer_norm(values, gain, shift):
    mean = jnp.mean(values, axis=-1, keepdims=True)
    centred = values - mean
    variance = jnp.mean(centred * centred, axis=-1, keepdims=True)
    return centred * lax.rsqrt(variance + EPS) * gain + shift


def kernel(
    idx, norms,
    grid_h, mesh_h, ge_h, pe_h, wg_h, wm_h, wr_h, wp_h, wn_h,
    mesh_out, grid_out,
    grid, halo, strips, mesh, ge, pe, wg, wm, wr, wp, wn,
    pre, src, total, node_pre, mid, near_out, near_in, far_out, far_in, gout, mout,
    load_sem, store_sem, halo_send, halo_recv, near_send, near_recv, far_send, far_recv, rounds,
):
    lat, lon = lax.axis_index("lat"), lax.axis_index("lon")
    me = lat * 16 + lon

    def device(p):
        return (lax.div(p, 16), lax.rem(p, 16))

    def neighbour(band, sector):
        return (lax.rem(lat + band + 8, 8), lax.rem(lon + sector + 16, 16))

    loads = [
        pltpu.make_async_copy(h, v, load_sem.at[i])
        for i, (h, v) in enumerate(
            ((grid_h, grid), (ge_h, ge), (mesh_h, mesh), (wg_h, wg), (wm_h, wm),
             (wp_h, wp), (pe_h, pe), (wr_h, wr), (wn_h, wn))
        )
    ]
    for copy in loads:
        copy.start()
    l_grid, l_ge, l_mesh, l_wg, l_wm, l_wp, l_pe, l_wr, l_wn = loads

    halo[pl.ds(HALO, HALO_PAD - HALO), :] = jnp.zeros((HALO_PAD - HALO, D), BF16)
    near_in[pl.ds(4 * NCAP, NCAP), :] = jnp.zeros((NCAP, D), BF16)
    near_in[pl.ds(NEAR, NEAR_PAD - NEAR), :] = jnp.zeros((NEAR_PAD - NEAR, D), BF16)
    far_in[pl.ds(0, FAR), :] = jnp.zeros((FAR, D), BF16)

    barrier = pltpu.get_barrier_semaphore()
    for band, sector, _, _ in SEGMENTS:
        pl.semaphore_signal(barrier, inc=1, device_id=neighbour(band, sector), device_id_type=MESH)
    for r in range(ROUNDS):
        pl.semaphore_signal(
            barrier, inc=1, device_id=device(lax.rem(me + DEVICES - 2**r, DEVICES)), device_id_type=MESH
        )

    def round_start(r):
        pl.semaphore_signal(
            rounds.at[r], inc=1, device_id=device(lax.rem(me + 2**r, DEVICES)), device_id_type=MESH
        )

    def round_end(r):
        pl.semaphore_wait(rounds.at[r], 1)

    lane = lax.broadcasted_iota(jnp.int32, (128, 128), 1)

    def offsets(first, b):
        row = idx[pl.ds(first + b, 1), :]
        return jnp.broadcast_to(row, (128, 128)).T - lane

    def pair(first, step):
        return jnp.concatenate([offsets(first, 2 * step), offsets(first, 2 * step + 1)], axis=0)

    def onehot(off, base, count):
        return jnp.concatenate(
            [jnp.where(off == base + 128 * k, 1.0, 0.0).astype(BF16) for k in range(count // 128)],
            axis=1,
        )

    def onehot_rows(first, step):
        row = jnp.concatenate(
            [idx[pl.ds(first + 2 * step, 1), :], idx[pl.ds(first + 2 * step + 1, 1), :]], axis=1
        )
        node = lax.broadcasted_iota(jnp.int32, (NODES, STEP), 0)
        return jnp.where(node == row, 1.0, 0.0).astype(BF16)

    def rows(step):
        return pl.ds(pl.multiple_of(step * STEP, STEP), STEP)

    def weight(ref, i):
        return ref[pl.ds(i * D, D), :]

    def norm(values, i):
        return layer_norm(values, norms[pl.ds(2 * i, 1), :], norms[pl.ds(2 * i + 1, 1), :])

    def loop(count, body):
        def run(step, carry):
            body(step)
            return carry

        lax.fori_loop(0, count, run, 0)

    l_grid.wait()
    spot = lax.broadcasted_iota(jnp.int32, (128, GRID), 0)
    cell = lax.broadcasted_iota(jnp.int32, (128, GRID), 1)
    wanted = jnp.where(spot < 64, 0, 60 - 1024) + lax.div(spot, 4) * 64 + lax.rem(spot, 4)
    strips[...] = dot(jnp.where(cell == wanted, 1.0, 0.0).astype(BF16), grid[...]).astype(BF16)

    sources = (
        grid.at[pl.ds(768, 256)], grid.at[pl.ds(0, 256)],
        strips.at[pl.ds(64, 64)], strips.at[pl.ds(0, 64)],
        strips.at[pl.ds(112, 16)], strips.at[pl.ds(48, 16)],
        strips.at[pl.ds(64, 16)], strips.at[pl.ds(0, 16)],
    )
    pl.semaphore_wait(barrier, len(SEGMENTS) + ROUNDS)
    halo_copies = [
        pltpu.make_async_remote_copy(
            src_ref=source,
            dst_ref=halo.at[pl.ds(first, count)],
            send_sem=halo_send.at[i],
            recv_sem=halo_recv.at[i],
            device_id=neighbour(band, sector),
            device_id_type=MESH,
        )
        for i, ((band, sector, first, count), source) in enumerate(zip(SEGMENTS, sources))
    ]
    for copy in halo_copies:
        copy.start()
    round_start(0)

    l_ge.wait()
    l_mesh.wait()
    l_wg.wait()

    def encode_first(step):
        here = rows(step)
        pos, row = pair(G_POS, step), pair(G_ROW, step)
        target = dot(onehot(row, 0, NODES), mesh[...]).astype(BF16)
        pre[here, :] = dot(ge[here, :], weight(wg, 0)) + dot(target, weight(wg, 2))
        src[here, :] = dot(onehot(pos, 0, GRID), grid[...]).astype(BF16)

    loop(3, encode_first)
    round_end(0)
    round_start(1)
    loop(2, lambda step: encode_first(step + 3))
    round_end(1)
    round_start(2)
    loop(2, lambda step: encode_first(step + 5))
    round_end(2)
    round_start(3)
    l_wm.wait()

    def node_first(step):
        here = rows(step)
        node_pre[here, :] = dot(mesh[here, :], weight(wm, 0))

    loop(2, node_first)
    total[...] = jnp.zeros((NODES, D), F32)
    for copy in halo_copies:
        copy.wait()
    round_end(3)
    round_start(4)

    def encode_last(step):
        here = rows(step)
        pos = pair(G_POS, step)
        arrived = dot(onehot(pos, GRID, HALO_PAD), halo[...]).astype(BF16)
        source = src[here, :] + arrived
        hidden = silu(pre[here, :] + dot(source, weight(wg, 1)))
        branch = norm(dot(hidden, weight(wg, 3)), 0)
        updated = (ge[here, :].astype(F32) + branch).astype(BF16)
        total[...] += dot(onehot_rows(G_ROW, step), updated)

    loop(4, encode_last)
    round_end(4)
    round_start(5)
    loop(3, lambda step: encode_last(step + 4))
    round_end(5)
    round_start(6)

    def node_last(step):
        here = rows(step)
        summed = total[here, :].astype(BF16)
        hidden = silu(node_pre[here, :] + dot(summed, weight(wm, 1)))
        branch = norm(dot(hidden, weight(wm, 2)), 1)
        mid[here, :] = (mesh[here, :].astype(F32) + branch).astype(BF16)

    loop(2, node_last)

    def near_pick(step):
        off = pair(NEAR_IDX, step)
        near_out[rows(step), :] = dot(onehot(off, 0, NODES), mid[...]).astype(BF16)

    def far_pick(step):
        off = pair(FAR_IDX, step)
        far_out[rows(step), :] = dot(onehot(off, 0, NODES), mid[...]).astype(BF16)

    loop(7, near_pick)
    round_end(6)
    near_copies = []
    for q in (0, 1, 2, 3, 5, 6, 7, 8):
        i = len(near_copies)
        near_copies.append(
            pltpu.make_async_remote_copy(
                src_ref=near_out.at[pl.ds(q * NCAP, NCAP)],
                dst_ref=near_in.at[pl.ds((8 - q) * NCAP, NCAP)],
                send_sem=near_send.at[i],
                recv_sem=near_recv.at[i],
                device_id=neighbour(q // 3 - 1, q % 3 - 1),
                device_id_type=MESH,
            )
        )
    for copy in near_copies:
        copy.start()
    loop(8, far_pick)

    slots = DEVICES // FAR_GROUPS

    def far_copy(k, g):
        other = lax.rem(me + k * FAR_MUL, DEVICES)
        return pltpu.make_async_remote_copy(
            src_ref=far_out.at[pl.ds(pl.multiple_of(other * FAR, FAR), FAR)],
            dst_ref=far_in.at[pl.ds(pl.multiple_of(k * FAR, FAR), FAR)],
            send_sem=far_send.at[g],
            recv_sem=far_recv.at[g],
            device_id=device(other),
            device_id_type=MESH,
        )

    for g in range(FAR_GROUPS):

        def send(k, carry, g=g):
            far_copy(k, g).start()
            return carry

        lax.fori_loop(max(g * slots, 1), (g + 1) * slots, send, 0)

    def far_group(g):
        first = max(g * slots, 1)
        span = pl.ds(first * FAR, ((g + 1) * slots - first) * FAR)
        return pltpu.make_async_remote_copy(
            src_ref=far_out.at[span],
            dst_ref=far_in.at[span],
            send_sem=far_send.at[g],
            recv_sem=far_recv.at[g],
            device_id=device(lax.rem(me + 1, DEVICES)),
            device_id_type=MESH,
        )

    l_wp.wait()
    l_pe.wait()

    def process_first(step):
        here = rows(step)
        pos, row = pair(P_POS, step), pair(P_ROW, step)
        target = dot(onehot(row, 0, NODES), mid[...]).astype(BF16)
        pre[here, :] = dot(pe[here, :], weight(wp, 0)) + dot(target, weight(wp, 2))
        src[here, :] = dot(onehot(pos, 0, NODES), mid[...]).astype(BF16)

    loop(8, process_first)
    l_wr.wait()

    def grid_step(step):
        here = rows(step)
        cells = grid[here, :]
        hidden = silu(dot(cells, weight(wr, 0)))
        branch = norm(dot(hidden, weight(wr, 1)), 2)
        gout[here, :] = (cells.astype(F32) + branch).astype(BF16)

    loop(4, grid_step)
    store_grid = pltpu.make_async_copy(gout, grid_out, store_sem.at[0])
    store_grid.start()
    l_wn.wait()

    def out_first(step):
        here = rows(step)
        node_pre[here, :] = dot(mid[here, :], weight(wn, 0))

    loop(2, out_first)
    total[...] = jnp.zeros((NODES, D), F32)

    for copy in near_copies:
        copy.wait()

    def take_near(step):
        here = rows(step)
        off = pair(P_POS, step)
        src[here, :] += dot(onehot(off, NODES, NEAR_PAD), near_in[...]).astype(BF16)

    loop(8, take_near)

    for g in range(FAR_GROUPS - 1):
        far_group(g).wait()

        def take_far(step, g=g):
            here = rows(step)
            off = pair(P_POS, step)
            table = far_in[pl.ds(g * slots * FAR, slots * FAR), :]
            hot = onehot(off, NODES + NEAR_PAD + g * slots * FAR, slots * FAR)
            src[here, :] += dot(hot, table).astype(BF16)

        loop(8, take_far)

    far_group(FAR_GROUPS - 1).wait()

    def process_last(step):
        here = rows(step)
        off = pair(P_POS, step)
        base = (FAR_GROUPS - 1) * slots * FAR
        table = far_in[pl.ds(base, slots * FAR), :]
        hot = onehot(off, NODES + NEAR_PAD + base, slots * FAR)
        source = src[here, :] + dot(hot, table).astype(BF16)
        hidden = silu(pre[here, :] + dot(source, weight(wp, 1)))
        branch = norm(dot(hidden, weight(wp, 3)), 3)
        updated = (pe[here, :].astype(F32) + branch).astype(BF16)
        total[...] += dot(onehot_rows(P_ROW, step), updated)

    loop(8, process_last)

    def out_last(step):
        here = rows(step)
        summed = total[here, :].astype(BF16)
        hidden = silu(node_pre[here, :] + dot(summed, weight(wn, 1)))
        branch = norm(dot(hidden, weight(wn, 2)), 4)
        mout[here, :] = (mid[here, :].astype(F32) + branch).astype(BF16)

    loop(2, out_last)
    store_mesh = pltpu.make_async_copy(mout, mesh_out, store_sem.at[1])
    store_mesh.start()
    store_mesh.wait()
    store_grid.wait()


def grid_spots(sender):
    i, j = sender // 72, sender % 72
    north, south = i < HW, i >= 20
    west, east = j < HW, j >= 68
    band = jnp.where(north, i, jnp.where(south, i - 20, i - HW))
    sector = jnp.where(west, j, jnp.where(east, j - 68, j - HW))
    edge = north | south
    side = west | east
    base = jnp.where(
        edge,
        jnp.where(
            side,
            1664 + 16 * (2 * south.astype(jnp.int32) + east.astype(jnp.int32)),
            jnp.where(north, 1024, 1280),
        ),
        jnp.where(west, 1536, jnp.where(east, 1600, 0)),
    )
    return base + band * jnp.where(side, 4, 64) + sector


def source_spots(sender, me):
    far = sender - (NODES + NEAR)
    other, slot = far // FAR, far % FAR
    place = ((me - other + DEVICES) * FAR_INV) % DEVICES
    return jnp.where(far >= 0, NODES + NEAR_PAD + place * FAR + slot, sender)


def node_rows(receiver, window):
    return jnp.where(receiver >= 0, window[:, None] * 128 + receiver, -1)


def body(
    grid_nodes, mesh_nodes, g2m_edges, mesh_edges, g2m_sender, g2m_receiver, g2m_window,
    mesh_sender, mesh_receiver, mesh_window, near_rows, far_rows,
    w_g2m_edge, w_mesh_node, w_grid_node, w_proc_edge, w_proc_node, norms,
):
    me = lax.axis_index("lat") * 16 + lax.axis_index("lon")
    near = jnp.concatenate(
        [near_rows.reshape(-1), jnp.full((NEAR_PAD - NEAR,), -1, jnp.int32)]
    ).reshape(-1, 128)
    idx = jnp.concatenate(
        [
            grid_spots(g2m_sender),
            node_rows(g2m_receiver, g2m_window),
            source_spots(mesh_sender, me),
            node_rows(mesh_receiver, mesh_window),
            near,
            far_rows.reshape(-1, 128),
        ],
        axis=0,
    )
    vmem = pl.BlockSpec(memory_space=pltpu.VMEM)
    any_space = pl.BlockSpec(memory_space=pl.ANY)

    def buf(count, dtype=BF16):
        return pltpu.VMEM((count, D), dtype)

    dma = pltpu.SemaphoreType.DMA
    mesh_out, grid_out = pl.pallas_call(
        kernel,
        out_shape=(
            jax.ShapeDtypeStruct((NODES, D), BF16),
            jax.ShapeDtypeStruct((GRID, D), BF16),
        ),
        in_specs=[vmem, vmem] + [any_space] * 9,
        out_specs=(any_space, any_space),
        scratch_shapes=[
            buf(GRID), buf(HALO_PAD), buf(128), buf(NODES), buf(G_EDGES), buf(P_EDGES),
            buf(4 * D), buf(3 * D), buf(2 * D), buf(4 * D), buf(3 * D),
            buf(P_EDGES, F32), buf(P_EDGES), buf(NODES, F32), buf(NODES, F32), buf(NODES),
            buf(NEAR_PAD), buf(NEAR_PAD), buf(DEVICES * FAR), buf(DEVICES * FAR),
            buf(GRID), buf(NODES),
            dma((9,)), dma((2,)), dma((8,)), dma((8,)), dma((8,)), dma((8,)),
            dma((FAR_GROUPS,)), dma((FAR_GROUPS,)), pltpu.SemaphoreType.REGULAR((ROUNDS,)),
        ],
        compiler_params=pltpu.CompilerParams(
            collective_id=0, has_side_effects=True, vmem_limit_bytes=52 * 2**20
        ),
    )(
        idx, norms.reshape(10, D),
        grid_nodes.reshape(GRID, D), mesh_nodes, g2m_edges.reshape(-1, D), mesh_edges.reshape(-1, D),
        w_g2m_edge.reshape(-1, D), w_mesh_node.reshape(-1, D), w_grid_node.reshape(-1, D),
        w_proc_edge.reshape(-1, D), w_proc_node.reshape(-1, D),
    )
    return mesh_out, grid_out.reshape(grid_nodes.shape)


def solution(mesh):
    both = ("lat", "lon")
    return jax.shard_map(
        body,
        mesh=mesh,
        in_specs=(
            P("lat", "lon", None), P(both, None), P(both, None, None), P(both, None, None),
            P(both, None), P(both, None), P(both), P(both, None), P(both, None), P(both),
            P(both, None, None), P(both, None, None),
            P(), P(), P(), P(), P(), P(),
        ),
        out_specs=(P(both, None), P("lat", "lon", None)),
        check_vma=False,
    )
```

```python
import jax
import jax.numpy as jnp
from jax import lax
from jax.experimental import pallas as pl
from jax.experimental.pallas import tpu as pltpu
from jax.sharding import PartitionSpec as P

HW = 4
EPS = 1e-05
D = 512
BF16 = jnp.bfloat16
F32 = jnp.float32
MESH = pl.DeviceIdType.MESH

GRID = 1024
HALO = 704
HALO_PAD = 768
NODES = 512
NCAP = 192
NEAR = 9 * NCAP
NEAR_ORDER = (1, 7, 3, 5, 0, 2, 6, 8)
NEAR_ROWS = 8 * NCAP
NEAR_GROUPS = ((0, 2), (2, 4), (4, 8))
FAR = 16
DEVICES = 128
G_EDGES = 1792
P_EDGES = 2048
E_STEP = 896
P_STEP = 1024
N_STEP = 512
C_STEP = 512
F_STEP = 1024

G_POS, G_ROW, P_POS, P_ROW = 0, 16, 32, 48
G_BLOCKS, P_BLOCKS = 14, 16

FAR_MUL = 77
FAR_INV = 5
FAR_GROUPS = 2
HOP = 12
HOPS = 10

SEGMENTS = (
    (1, 0, 0, 256),
    (-1, 0, 256, 256),
    (0, 1, 512, 64),
    (0, -1, 576, 64),
    (1, 1, 640, 16),
    (1, -1, 656, 16),
    (-1, 1, 672, 16),
    (-1, -1, 688, 16),
)


def dot(a, b):
    return jnp.dot(a, b, preferred_element_type=F32)


def silu(v):
    half = 0.5 * v
    return (half + half * jnp.tanh(half)).astype(BF16)


def layer_norm(values, gain, shift):
    mean = jnp.mean(values, axis=-1, keepdims=True)
    centred = values - mean
    variance = jnp.mean(centred * centred, axis=-1, keepdims=True)
    return centred * lax.rsqrt(variance + EPS) * gain + shift


def grid_spots(sender):
    i = (sender * 14564) >> 20
    j = sender - 72 * i
    north, south = i < HW, i >= 20
    west, east = j < HW, j >= 68
    edge, side = north | south, west | east
    band = jnp.where(north, i, jnp.where(south, i - 20, i - HW))
    sector = jnp.where(west, j, jnp.where(east, j - 68, j - HW))
    corner = 1664 + jnp.where(south, 32, 0) + jnp.where(east, 16, 0)
    base = jnp.where(
        edge,
        jnp.where(side, corner, jnp.where(north, 1024, 1280)),
        jnp.where(west, 1536, jnp.where(east, 1600, 0)),
    )
    return base + band * jnp.where(side, 4, 64) + sector


def source_spots(sender, me):
    far = sender - (NODES + NEAR)
    place = (((me - (far >> 4)) & (DEVICES - 1)) * FAR_INV) & (DEVICES - 1)
    near = sender - NODES
    q = (near * 10923) >> 21
    order = jnp.zeros_like(q)
    for i, position in enumerate(NEAR_ORDER):
        order = jnp.where(q == position, i, order)
    near_spot = NODES + order * NCAP + near - q * NCAP
    far_spot = NODES + NEAR_ROWS + place * FAR + (far & (FAR - 1))
    return jnp.where(far >= 0, far_spot, jnp.where(near >= 0, near_spot, sender))


def kernel(
    g_window, p_window,
    gs_h, gr_h, ps_h, pr_h, near_h, far_h, norms_h,
    grid_h, mesh_h, ge_h, pe_h, wg_h, wm_h, wr_h, wp_h, wn_h,
    mesh_out, grid_out,
    gs, gr, ps, pr, near, far, norms, idx,
    grid, halo, strips, mesh, ge, pe, wg, wm, wr, wp, wn,
    pre, src, total, node_pre, mid, near_out, near_in, far_out, far_in, gout, mout,
    far_hot, table,
    load_sem, store_sem, halo_send, halo_recv, near_send, near_recv, far_send, far_recv, round_sem,
):
    lat, lon = lax.axis_index("lat"), lax.axis_index("lon")
    me = lat * 16 + lon

    def device(p):
        return (lax.div(p, 16), lax.rem(p, 16))

    def neighbour(band, sector):
        return (lax.rem(lat + band + 8, 8), lax.rem(lon + sector + 16, 16))

    loads = [
        pltpu.make_async_copy(h, v, load_sem.at[i])
        for i, (h, v) in enumerate(
            ((grid_h, grid), (gs_h, gs), (gr_h, gr), (mesh_h, mesh), (ge_h, ge), (wg_h, wg),
             (ps_h, ps), (pr_h, pr), (near_h, near), (far_h, far), (norms_h, norms), (wm_h, wm),
             (wp_h, wp), (pe_h, pe), (wr_h, wr), (wn_h, wn))
        )
    ]
    for copy in loads:
        copy.start()
    l_grid, l_gs, l_gr, l_mesh, l_ge, l_wg = loads[:6]
    l_small, (l_wm, l_wp, l_pe, l_wr, l_wn) = loads[6:11], loads[11:]

    halo[pl.ds(HALO, HALO_PAD - HALO), :] = jnp.zeros((HALO_PAD - HALO, D), BF16)
    far_in[pl.ds(0, FAR), :] = jnp.zeros((FAR, D), BF16)

    barrier = pltpu.get_barrier_semaphore()

    def greet(to):
        pl.semaphore_signal(barrier, inc=1, device_id=to, device_id_type=MESH)

    for band, sector, _, _ in SEGMENTS:
        greet(neighbour(band, sector))
    steps_back = [HOP * j for j in range(1, HOPS + 1)] + list(range(1, HOP))
    for back in steps_back:
        greet(device(lax.rem(me + DEVICES - back, DEVICES)))

    lane = lax.broadcasted_iota(jnp.int32, (128, 128), 1)

    def offsets(first, b):
        row = idx[pl.ds(first + b, 1), :]
        return jnp.broadcast_to(row, (128, 128)).T - lane

    def columns(first, step, count):
        blocks = count // 128
        return jnp.concatenate([offsets(first, step * blocks + b) for b in range(blocks)], axis=0)

    def node_rows(receiver, window, first, count):
        for b in range(count):
            row = receiver[pl.ds(b, 1), :]
            idx[pl.ds(first + b, 1), :] = jnp.where(row >= 0, row + 128 * window[b], -1)

    def onehot(off, base, count):
        return jnp.concatenate(
            [jnp.where(off == base + 128 * k, 1.0, 0.0).astype(BF16) for k in range(count // 128)],
            axis=1,
        )

    def onehot_rows(first, step, count):
        blocks = count // 128
        row = jnp.concatenate(
            [idx[pl.ds(first + step * blocks + b, 1), :] for b in range(blocks)], axis=1
        )
        node = lax.broadcasted_iota(jnp.int32, (NODES, count), 0)
        return jnp.where(node == row, 1.0, 0.0).astype(BF16)

    def rows(step, count):
        return pl.ds(pl.multiple_of(step * count, count), count)

    def weight(ref, i):
        return ref[pl.ds(i * D, D), :]

    def norm(values, i):
        return layer_norm(values, norms[i, pl.ds(0, 1), :], norms[i, pl.ds(1, 1), :])

    def loop(count, body):
        def run(step, carry):
            body(step)
            return carry

        lax.fori_loop(0, count, run, 0)

    l_grid.wait()
    spot = lax.broadcasted_iota(jnp.int32, (128, GRID), 0)
    cell = lax.broadcasted_iota(jnp.int32, (128, GRID), 1)
    wanted = jnp.where(spot < 64, 0, 60 - 1024) + lax.div(spot, 4) * 64 + lax.rem(spot, 4)
    strips[...] = dot(jnp.where(cell == wanted, 1.0, 0.0).astype(BF16), grid[...]).astype(BF16)

    sources = (
        grid.at[pl.ds(768, 256)], grid.at[pl.ds(0, 256)],
        strips.at[pl.ds(64, 64)], strips.at[pl.ds(0, 64)],
        strips.at[pl.ds(112, 16)], strips.at[pl.ds(48, 16)],
        strips.at[pl.ds(64, 16)], strips.at[pl.ds(0, 16)],
    )
    pl.semaphore_wait(barrier, len(SEGMENTS) + len(steps_back))
    halo_copies = [
        pltpu.make_async_remote_copy(
            src_ref=source,
            dst_ref=halo.at[pl.ds(first, count)],
            send_sem=halo_send.at[i],
            recv_sem=halo_recv.at[i],
            device_id=neighbour(band, sector),
            device_id_type=MESH,
        )
        for i, ((band, sector, first, count), source) in enumerate(zip(SEGMENTS, sources))
    ]
    for copy in halo_copies:
        copy.start()
    for ahead in range(1, HOP):
        pl.semaphore_signal(
            round_sem, inc=1, device_id=device(lax.rem(me + ahead, DEVICES)), device_id_type=MESH
        )

    l_gs.wait()
    l_gr.wait()
    idx[pl.ds(G_POS, G_BLOCKS), :] = grid_spots(gs[...])
    node_rows(gr, g_window, G_ROW, G_BLOCKS)
    l_ge.wait()
    l_mesh.wait()
    l_wg.wait()

    def encode_first(step):
        here = rows(step, E_STEP)
        row = columns(G_ROW, step, E_STEP)
        target = dot(onehot(row, 0, NODES), mesh[...]).astype(BF16)
        pos = columns(G_POS, step, E_STEP)
        source = dot(onehot(pos, 0, GRID), grid[...]).astype(BF16)
        pre[here, :] = (
            dot(ge[here, :], weight(wg, 0)) + dot(target, weight(wg, 2)) + dot(source, weight(wg, 1))
        )

    loop(G_EDGES // E_STEP, encode_first)
    for copy in l_small:
        copy.wait()
    idx[pl.ds(P_POS, P_BLOCKS), :] = source_spots(ps[...], me)
    node_rows(pr, p_window, P_ROW, P_BLOCKS)

    edge = lax.broadcasted_iota(jnp.int32, (F_STEP, DEVICES), 0)
    lane_of = lax.broadcasted_iota(jnp.int32, (F_STEP, DEVICES), 1)
    of_slot = jnp.where(
        (lax.broadcasted_iota(jnp.int32, (F_STEP, FAR), 0) & (FAR - 1))
        == lax.broadcasted_iota(jnp.int32, (F_STEP, FAR), 1), 1.0, 0.0
    )
    spread = jnp.ones((FAR, 128), BF16)

    def far_spots(step):
        of_list = jnp.where((edge >> 4) + step * (F_STEP // FAR) == lane_of, 1.0, 0.0).astype(BF16)

        def expand(part):
            mine = lax.dot_general(
                of_list, part.astype(F32).astype(BF16), (((1,), (1,)), ((), ())),
                preferred_element_type=F32,
            )
            return dot((mine * of_slot).astype(BF16), spread)

        lists = far[0]
        off = 16.0 * expand(lists >> 4) + expand(lists & 15) - lane_of.astype(F32)
        far_hot[rows(step, F_STEP), :] = jnp.concatenate(
            [jnp.where(off == 128.0 * k, 1.0, 0.0).astype(BF16) for k in range(NODES // 128)], axis=1
        )

    loop(DEVICES * FAR // F_STEP, far_spots)
    l_wm.wait()

    def node_first(step):
        here = rows(step, N_STEP)
        node_pre[here, :] = dot(mesh[here, :], weight(wm, 0))

    loop(NODES // N_STEP, node_first)
    total[...] = jnp.zeros((NODES, D), F32)
    for copy in halo_copies:
        copy.wait()

    table[pl.ds(0, HALO_PAD), :] = dot(halo[...], weight(wg, 1)).astype(BF16)

    def encode_last(step):
        here = rows(step, E_STEP)
        pos = columns(G_POS, step, E_STEP)
        hidden = silu(pre[here, :] + dot(onehot(pos, GRID, HALO_PAD), table[pl.ds(0, HALO_PAD), :]))
        branch = norm(dot(hidden, weight(wg, 3)), 0)
        updated = (ge[here, :].astype(F32) + branch).astype(BF16)
        total[...] += dot(onehot_rows(G_ROW, step, E_STEP), updated)

    loop(G_EDGES // E_STEP, encode_last)

    def node_last(step):
        here = rows(step, N_STEP)
        summed = total[here, :].astype(BF16)
        hidden = silu(node_pre[here, :] + dot(summed, weight(wm, 1)))
        branch = norm(dot(hidden, weight(wm, 2)), 1)
        mid[here, :] = (mesh[here, :].astype(F32) + branch).astype(BF16)

    loop(NODES // N_STEP, node_last)

    def far_pick(step):
        here = rows(step, F_STEP)
        far_out[here, :] = dot(far_hot[here, :], mid[...]).astype(BF16)

    loop(DEVICES * FAR // F_STEP, far_pick)
    pl.semaphore_wait(round_sem, HOP - 1)

    slots = DEVICES // FAR_GROUPS

    def far_copy(k, g):
        other = lax.rem(me + k * FAR_MUL, DEVICES)
        return pltpu.make_async_remote_copy(
            src_ref=far_out.at[pl.ds(pl.multiple_of(other * FAR, FAR), FAR)],
            dst_ref=far_in.at[pl.ds(pl.multiple_of(k * FAR, FAR), FAR)],
            send_sem=far_send.at[g],
            recv_sem=far_recv.at[g],
            device_id=device(other),
            device_id_type=MESH,
        )

    for g in range(FAR_GROUPS):

        def send(k, carry, g=g):
            far_copy(k, g).start()
            return carry

        lax.fori_loop(max(g * slots, 1), (g + 1) * slots, send, 0)

    def near_columns(q):
        row = near[q]
        first = jnp.broadcast_to(row[:, :128], (128, 128)).T - lane
        second = jnp.broadcast_to(row[:, 64:], (128, 128)).T - lane
        return jnp.concatenate([first, second[64:]], axis=0)

    def near_pick(half):
        off = jnp.concatenate([near_columns(5 * half + i) for i in range(4)], axis=0)
        picked = dot(onehot(off, 0, NODES), mid[...]).astype(BF16)
        near_out[pl.ds(pl.multiple_of(half * 4 * NCAP, 4 * NCAP), 4 * NCAP), :] = picked

    loop(2, near_pick)
    near_copies = []
    for i, q in enumerate(NEAR_ORDER):
        own = 8 - q
        near_copies.append(
            pltpu.make_async_remote_copy(
                src_ref=near_out.at[pl.ds((own - own // 5) * NCAP, NCAP)],
                dst_ref=near_in.at[pl.ds(i * NCAP, NCAP)],
                send_sem=near_send.at[i],
                recv_sem=near_recv.at[i],
                device_id=neighbour(own // 3 - 1, own % 3 - 1),
                device_id_type=MESH,
            )
        )
    for copy in near_copies:
        copy.start()

    def far_group(g):
        first = max(g * slots, 1)
        span = pl.ds(first * FAR, ((g + 1) * slots - first) * FAR)
        return pltpu.make_async_remote_copy(
            src_ref=far_out.at[span],
            dst_ref=far_in.at[span],
            send_sem=far_send.at[g],
            recv_sem=far_recv.at[g],
            device_id=device(lax.rem(me + 1, DEVICES)),
            device_id_type=MESH,
        )

    l_wp.wait()
    l_pe.wait()

    def process_first(step):
        here = rows(step, P_STEP)
        pos, row = columns(P_POS, step, P_STEP), columns(P_ROW, step, P_STEP)
        target = dot(onehot(row, 0, NODES), mid[...]).astype(BF16)
        pre[here, :] = dot(pe[here, :], weight(wp, 0)) + dot(target, weight(wp, 2))
        src[here, :] = dot(onehot(pos, 0, NODES), mid[...]).astype(BF16)

    loop(P_EDGES // P_STEP, process_first)
    l_wr.wait()

    def grid_step(step):
        here = rows(step, C_STEP)
        cells = grid[here, :]
        hidden = silu(dot(cells, weight(wr, 0)))
        branch = norm(dot(hidden, weight(wr, 1)), 2)
        gout[here, :] = (cells.astype(F32) + branch).astype(BF16)

    loop(GRID // C_STEP, grid_step)
    store_grid = pltpu.make_async_copy(gout, grid_out, store_sem.at[0])
    store_grid.start()
    l_wn.wait()

    def out_first(step):
        here = rows(step, N_STEP)
        node_pre[here, :] = dot(mid[here, :], weight(wn, 0))

    loop(NODES // N_STEP, out_first)
    total[...] = jnp.zeros((NODES, D), F32)

    far_base = NODES + NEAR_ROWS

    def take(count, base, arrived):
        def step_of(step):
            here = rows(step, P_STEP)
            off = columns(P_POS, step, P_STEP)
            src[here, :] += dot(onehot(off, base, count), arrived[...]).astype(BF16)

        loop(P_EDGES // P_STEP, step_of)

    def near_part(group):
        first, last = group
        for copy in near_copies[first:last]:
            copy.wait()
        return pl.ds(first * NCAP, (last - first) * NCAP)

    for g in range(FAR_GROUPS):
        far_group(g).wait()
        first = g * slots * FAR
        take(slots * FAR, far_base + first, far_in.at[pl.ds(first, slots * FAR)])
    for group in NEAR_GROUPS[:-1]:
        part = near_part(group)
        take(part.size, NODES + part.start, near_in.at[part])

    def project(step):
        here = rows(step, P_STEP)
        pre[here, :] += dot(src[here, :], weight(wp, 1))

    loop(P_EDGES // P_STEP, project)
    last = near_part(NEAR_GROUPS[-1])
    table[...] = dot(near_in[last, :], weight(wp, 1)).astype(BF16)

    def process_last(step):
        here = rows(step, P_STEP)
        off = columns(P_POS, step, P_STEP)
        hidden = silu(pre[here, :] + dot(onehot(off, NODES + last.start, last.size), table[...]))
        branch = norm(dot(hidden, weight(wp, 3)), 3)
        updated = (pe[here, :].astype(F32) + branch).astype(BF16)
        total[...] += dot(onehot_rows(P_ROW, step, P_STEP), updated)

    loop(P_EDGES // P_STEP, process_last)

    def out_last(step):
        here = rows(step, N_STEP)
        summed = total[here, :].astype(BF16)
        hidden = silu(node_pre[here, :] + dot(summed, weight(wn, 1)))
        branch = norm(dot(hidden, weight(wn, 2)), 4)
        mout[here, :] = (mid[here, :].astype(F32) + branch).astype(BF16)

    loop(NODES // N_STEP, out_last)
    store_mesh = pltpu.make_async_copy(mout, mesh_out, store_sem.at[1])
    store_mesh.start()
    store_mesh.wait()
    store_grid.wait()


def body(
    grid_nodes, mesh_nodes, g2m_edges, mesh_edges, g2m_sender, g2m_receiver, g2m_window,
    mesh_sender, mesh_receiver, mesh_window, near_rows, far_rows,
    w_g2m_edge, w_mesh_node, w_grid_node, w_proc_edge, w_proc_node, norms,
):
    smem = pl.BlockSpec(memory_space=pltpu.SMEM)
    any_space = pl.BlockSpec(memory_space=pl.ANY)

    def buf(count, dtype=BF16):
        return pltpu.VMEM((count, D), dtype)

    def ints(*shape):
        return pltpu.VMEM(shape, jnp.int32)

    dma = pltpu.SemaphoreType.DMA
    mesh_out, grid_out = pl.pallas_call(
        kernel,
        out_shape=(
            jax.ShapeDtypeStruct((NODES, D), BF16),
            jax.ShapeDtypeStruct((GRID, D), BF16),
        ),
        in_specs=[smem, smem] + [any_space] * 16,
        out_specs=(any_space, any_space),
        scratch_shapes=[
            ints(G_BLOCKS, 128), ints(G_BLOCKS, 128), ints(P_BLOCKS, 128), ints(P_BLOCKS, 128),
            ints(9, 1, NCAP), ints(1, FAR, DEVICES), pltpu.VMEM((5, 2, D), F32), ints(64, 128),
            buf(GRID), buf(HALO_PAD), buf(128), buf(NODES), buf(G_EDGES), buf(P_EDGES),
            buf(4 * D), buf(3 * D), buf(2 * D), buf(4 * D), buf(3 * D),
            buf(P_EDGES, F32), buf(P_EDGES), buf(NODES, F32), buf(NODES, F32), buf(NODES),
            buf(NEAR_ROWS), buf(NEAR_ROWS), buf(DEVICES * FAR), buf(DEVICES * FAR),
            buf(GRID), buf(NODES), buf(DEVICES * FAR), buf(HALO_PAD),
            dma((16,)), dma((2,)), dma((8,)), dma((8,)), dma((8,)), dma((8,)),
            dma((FAR_GROUPS,)), dma((FAR_GROUPS,)), pltpu.SemaphoreType.REGULAR,
        ],
        compiler_params=pltpu.CompilerParams(
            collective_id=0, has_side_effects=True, vmem_limit_bytes=63 * 2**20
        ),
    )(
        g2m_window, mesh_window,
        g2m_sender, g2m_receiver, mesh_sender, mesh_receiver, near_rows.transpose(1, 0, 2), far_rows.transpose(0, 2, 1), norms,
        grid_nodes.reshape(GRID, D), mesh_nodes, g2m_edges.reshape(-1, D), mesh_edges.reshape(-1, D),
        w_g2m_edge.reshape(-1, D), w_mesh_node.reshape(-1, D), w_grid_node.reshape(-1, D),
        w_proc_edge.reshape(-1, D), w_proc_node.reshape(-1, D),
    )
    return mesh_out, grid_out.reshape(grid_nodes.shape)


def solution(mesh):
    both = ("lat", "lon")
    return jax.shard_map(
        body,
        mesh=mesh,
        in_specs=(
            P("lat", "lon", None), P(both, None), P(both, None, None), P(both, None, None),
            P(both, None), P(both, None), P(both), P(both, None), P(both, None), P(both),
            P(both, None, None), P(both, None, None),
            P(), P(), P(), P(), P(), P(),
        ),
        out_specs=(P(both, None), P("lat", "lon", None)),
        check_vma=False,
    )
```

```python
import jax
import jax.numpy as jnp
from jax import lax
from jax.experimental import pallas as pl
from jax.experimental.pallas import tpu as pltpu
from jax.sharding import PartitionSpec as P

HW = 4
EPS = 1e-05
D = 512
BF16 = jnp.bfloat16
F32 = jnp.float32
MESH = pl.DeviceIdType.MESH

GRID = 1024
HALO = 704
HALO_PAD = 768
NODES = 512
NCAP = 192
NEAR = 9 * NCAP
NEAR_ORDER = (1, 7, 3, 5, 0, 2, 6, 8)
NEAR_ROWS = 8 * NCAP
NEAR_GROUPS = ((0, 2), (2, 6), (6, 8))
LAST = (NEAR_GROUPS[-1][1] - NEAR_GROUPS[-1][0]) * NCAP
FAR = 16
DEVICES = 128
G_EDGES = 1792
P_EDGES = 2048
E_STEP = 1792
P_STEP = 2048
N_STEP = 512
C_STEP = 512
F_STEP = 1024

G_POS, G_ROW, P_POS, P_ROW = 0, 16, 32, 48
G_BLOCKS, P_BLOCKS = 14, 16

FAR_MUL = 77
FAR_INV = 5
FAR_GROUPS = 2
HOP = 12
HOPS = 10

SEGMENTS = (
    (1, 0, 0, 256),
    (-1, 0, 256, 256),
    (0, 1, 512, 64),
    (0, -1, 576, 64),
    (1, 1, 640, 16),
    (1, -1, 656, 16),
    (-1, 1, 672, 16),
    (-1, -1, 688, 16),
)


def dot(a, b):
    return jnp.dot(a, b, preferred_element_type=F32)


def silu(v):
    half = 0.5 * v
    return (half + half * jnp.tanh(half)).astype(BF16)


def layer_norm(values, gain, shift):
    mean = jnp.mean(values, axis=-1, keepdims=True)
    centred = values - mean
    variance = jnp.mean(centred * centred, axis=-1, keepdims=True)
    return centred * lax.rsqrt(variance + EPS) * gain + shift


def grid_spots(sender):
    i = (sender * 14564) >> 20
    j = sender - 72 * i
    north, south = i < HW, i >= 20
    west, east = j < HW, j >= 68
    edge, side = north | south, west | east
    band = jnp.where(north, i, jnp.where(south, i - 20, i - HW))
    sector = jnp.where(west, j, jnp.where(east, j - 68, j - HW))
    corner = 1664 + jnp.where(south, 32, 0) + jnp.where(east, 16, 0)
    base = jnp.where(
        edge,
        jnp.where(side, corner, jnp.where(north, 1024, 1280)),
        jnp.where(west, 1536, jnp.where(east, 1600, 0)),
    )
    return base + band * jnp.where(side, 4, 64) + sector


def source_spots(sender, me):
    far = sender - (NODES + NEAR)
    place = (((me - (far >> 4)) & (DEVICES - 1)) * FAR_INV) & (DEVICES - 1)
    near = sender - NODES
    q = (near * 10923) >> 21
    order = jnp.zeros_like(q)
    for i, position in enumerate(NEAR_ORDER):
        order = jnp.where(q == position, i, order)
    near_spot = NODES + order * NCAP + near - q * NCAP
    far_spot = NODES + NEAR_ROWS + place * FAR + (far & (FAR - 1))
    return jnp.where(far >= 0, far_spot, jnp.where(near >= 0, near_spot, sender))


def kernel(
    g_window, p_window,
    gs_h, gr_h, ps_h, pr_h, near_h, far_h, norms_h,
    grid_h, mesh_h, ge_h, pe_h, wg_h, wm_h, wr_h, wp_h, wn_h,
    mesh_out, grid_out,
    gs, gr, ps, pr, near, far, norms, idx,
    grid, halo, strips, mesh, ge, pe, wg, wm, wr, wp, wn,
    pre, src, total, node_pre, mid, near_out, near_in, far_out, far_in,
    far_hot, table, cells, last_hot, sum_hot,
    load_sem, halo_send, halo_recv, near_send, near_recv, far_send, far_recv, round_sem,
):
    lat, lon = lax.axis_index("lat"), lax.axis_index("lon")
    me = lat * 16 + lon

    def device(p):
        return (lax.div(p, 16), lax.rem(p, 16))

    def neighbour(band, sector):
        return (lax.rem(lat + band + 8, 8), lax.rem(lon + sector + 16, 16))

    loads = [
        pltpu.make_async_copy(h, v, load_sem.at[i])
        for i, (h, v) in enumerate(
            ((grid_h, grid), (gs_h, gs), (gr_h, gr), (mesh_h, mesh), (ge_h, ge), (wg_h, wg),
             (ps_h, ps), (pr_h, pr), (near_h, near), (far_h, far), (norms_h, norms), (wm_h, wm),
             (wp_h, wp), (pe_h, pe), (wr_h, wr), (wn_h, wn))
        )
    ]
    for copy in loads:
        copy.start()
    l_grid, l_gs, l_gr, l_mesh, l_ge, l_wg = loads[:6]
    l_small, (l_wm, l_wp, l_pe, l_wr, l_wn) = loads[6:11], loads[11:]

    halo[pl.ds(HALO, HALO_PAD - HALO), :] = jnp.zeros((HALO_PAD - HALO, D), BF16)
    far_in[pl.ds(0, FAR), :] = jnp.zeros((FAR, D), BF16)

    barrier = pltpu.get_barrier_semaphore()

    def greet(to):
        pl.semaphore_signal(barrier, inc=1, device_id=to, device_id_type=MESH)

    for band, sector, _, _ in SEGMENTS:
        greet(neighbour(band, sector))
    steps_back = [HOP * j for j in range(1, HOPS + 1)] + list(range(1, HOP))
    for back in steps_back:
        greet(device(lax.rem(me + DEVICES - back, DEVICES)))

    lane = lax.broadcasted_iota(jnp.int32, (128, 128), 1)

    def offsets(first, b):
        row = idx[pl.ds(first + b, 1), :]
        return jnp.broadcast_to(row, (128, 128)).T - lane

    def columns(first, step, count):
        blocks = count // 128
        return jnp.concatenate([offsets(first, step * blocks + b) for b in range(blocks)], axis=0)

    def node_rows(receiver, window, first, count):
        for b in range(count):
            row = receiver[pl.ds(b, 1), :]
            idx[pl.ds(first + b, 1), :] = jnp.where(row >= 0, row + 128 * window[b], -1)

    def onehot(off, base, count):
        return jnp.concatenate(
            [jnp.where(off == base + 128 * k, 1.0, 0.0).astype(BF16) for k in range(count // 128)],
            axis=1,
        )

    def onehot_rows(first, step, count):
        blocks = count // 128
        row = jnp.concatenate(
            [idx[pl.ds(first + step * blocks + b, 1), :] for b in range(blocks)], axis=1
        )
        node = lax.broadcasted_iota(jnp.int32, (NODES, count), 0)
        return jnp.where(node == row, 1.0, 0.0).astype(BF16)

    def rows(step, count):
        return pl.ds(pl.multiple_of(step * count, count), count)

    def weight(ref, i):
        return ref[pl.ds(i * D, D), :]

    def norm(values, i):
        return layer_norm(values, norms[i, pl.ds(0, 1), :], norms[i, pl.ds(1, 1), :])

    def loop(count, body):
        def run(step, carry):
            body(step)
            return carry

        lax.fori_loop(0, count, run, 0)

    l_grid.wait()
    spot = lax.broadcasted_iota(jnp.int32, (128, GRID), 0)
    cell = lax.broadcasted_iota(jnp.int32, (128, GRID), 1)
    wanted = jnp.where(spot < 64, 0, 60 - 1024) + lax.div(spot, 4) * 64 + lax.rem(spot, 4)
    strips[...] = dot(jnp.where(cell == wanted, 1.0, 0.0).astype(BF16), grid[...]).astype(BF16)

    sources = (
        grid.at[pl.ds(768, 256)], grid.at[pl.ds(0, 256)],
        strips.at[pl.ds(64, 64)], strips.at[pl.ds(0, 64)],
        strips.at[pl.ds(112, 16)], strips.at[pl.ds(48, 16)],
        strips.at[pl.ds(64, 16)], strips.at[pl.ds(0, 16)],
    )
    pl.semaphore_wait(barrier, len(SEGMENTS) + len(steps_back))
    halo_copies = [
        pltpu.make_async_remote_copy(
            src_ref=source,
            dst_ref=halo.at[pl.ds(first, count)],
            send_sem=halo_send.at[i],
            recv_sem=halo_recv.at[i],
            device_id=neighbour(band, sector),
            device_id_type=MESH,
        )
        for i, ((band, sector, first, count), source) in enumerate(zip(SEGMENTS, sources))
    ]
    for copy in halo_copies:
        copy.start()
    for ahead in range(1, HOP):
        pl.semaphore_signal(
            round_sem, inc=1, device_id=device(lax.rem(me + ahead, DEVICES)), device_id_type=MESH
        )

    l_gs.wait()
    l_gr.wait()
    idx[pl.ds(G_POS, G_BLOCKS), :] = grid_spots(gs[...])
    node_rows(gr, g_window, G_ROW, G_BLOCKS)
    l_ge.wait()
    l_mesh.wait()
    l_wg.wait()

    table[pl.ds(0, NODES), :] = dot(mesh[...], weight(wg, 2)).astype(BF16)
    cells[...] = dot(grid[...], weight(wg, 1)).astype(BF16)

    def encode_first(step):
        here = rows(step, E_STEP)
        row = columns(G_ROW, step, E_STEP)
        pos = columns(G_POS, step, E_STEP)
        pre[here, :] = (
            dot(ge[here, :], weight(wg, 0))
            + dot(onehot(row, 0, NODES), table[pl.ds(0, NODES), :])
            + dot(onehot(pos, 0, GRID), cells[...])
        )

    loop(G_EDGES // E_STEP, encode_first)
    for copy in l_small:
        copy.wait()
    idx[pl.ds(P_POS, P_BLOCKS), :] = source_spots(ps[...], me)
    node_rows(pr, p_window, P_ROW, P_BLOCKS)

    edge = lax.broadcasted_iota(jnp.int32, (F_STEP, DEVICES), 0)
    lane_of = lax.broadcasted_iota(jnp.int32, (F_STEP, DEVICES), 1)
    of_slot = jnp.where(
        (lax.broadcasted_iota(jnp.int32, (F_STEP, FAR), 0) & (FAR - 1))
        == lax.broadcasted_iota(jnp.int32, (F_STEP, FAR), 1), 1.0, 0.0
    )
    spread = jnp.ones((FAR, 128), BF16)

    def far_spots(step):
        place = (edge >> 4) + step * (F_STEP // FAR)
        of_list = jnp.where(((me + place * FAR_MUL) & (DEVICES - 1)) == lane_of, 1.0, 0.0).astype(BF16)

        def expand(part):
            mine = lax.dot_general(
                of_list, part.astype(F32).astype(BF16), (((1,), (1,)), ((), ())),
                preferred_element_type=F32,
            )
            return dot((mine * of_slot).astype(BF16), spread)

        lists = far[0]
        off = 16.0 * expand(lists >> 4) + expand(lists & 15) - lane_of.astype(F32)
        far_hot[rows(step, F_STEP), :] = jnp.concatenate(
            [jnp.where(off == 128.0 * k, 1.0, 0.0).astype(BF16) for k in range(NODES // 128)], axis=1
        )

    loop(DEVICES * FAR // F_STEP, far_spots)
    l_wm.wait()

    def node_first(step):
        here = rows(step, N_STEP)
        node_pre[here, :] = dot(mesh[here, :], weight(wm, 0))

    loop(NODES // N_STEP, node_first)
    total[...] = jnp.zeros((NODES, D), F32)
    for copy in halo_copies:
        copy.wait()

    table[pl.ds(0, HALO_PAD), :] = dot(halo[...], weight(wg, 1)).astype(BF16)

    def encode_last(step):
        here = rows(step, E_STEP)
        pos = columns(G_POS, step, E_STEP)
        hidden = silu(pre[here, :] + dot(onehot(pos, GRID, HALO_PAD), table[pl.ds(0, HALO_PAD), :]))
        branch = norm(dot(hidden, weight(wg, 3)), 0)
        updated = (ge[here, :].astype(F32) + branch).astype(BF16)
        total[...] += dot(onehot_rows(G_ROW, step, E_STEP), updated)

    loop(G_EDGES // E_STEP, encode_last)

    def node_last(step):
        here = rows(step, N_STEP)
        summed = total[here, :].astype(BF16)
        hidden = silu(node_pre[here, :] + dot(summed, weight(wm, 1)))
        branch = norm(dot(hidden, weight(wm, 2)), 1)
        mid[here, :] = (mesh[here, :].astype(F32) + branch).astype(BF16)

    loop(NODES // N_STEP, node_last)

    def far_pick(step):
        here = rows(step, F_STEP)
        far_out[here, :] = dot(far_hot[here, :], mid[...]).astype(BF16)

    slots = DEVICES // FAR_GROUPS

    def far_copy(k, g):
        there = pl.ds(pl.multiple_of(k * FAR, FAR), FAR)
        return pltpu.make_async_remote_copy(
            src_ref=far_out.at[there],
            dst_ref=far_in.at[there],
            send_sem=far_send.at[g],
            recv_sem=far_recv.at[g],
            device_id=device(lax.rem(me + k * FAR_MUL, DEVICES)),
            device_id_type=MESH,
        )

    for g in range(FAR_GROUPS):
        far_pick(g)
        if g == 0:
            pl.semaphore_wait(round_sem, HOP - 1)

        def send(k, carry, g=g):
            far_copy(k, g).start()
            return carry

        lax.fori_loop(max(g * slots, 1), (g + 1) * slots, send, 0)

    def near_columns(q):
        row = near[q]
        first = jnp.broadcast_to(row[:, :128], (128, 128)).T - lane
        second = jnp.broadcast_to(row[:, 64:], (128, 128)).T - lane
        return jnp.concatenate([first, second[64:]], axis=0)

    def near_pick(half):
        off = jnp.concatenate([near_columns(5 * half + i) for i in range(4)], axis=0)
        picked = dot(onehot(off, 0, NODES), mid[...]).astype(BF16)
        near_out[pl.ds(pl.multiple_of(half * 4 * NCAP, 4 * NCAP), 4 * NCAP), :] = picked

    loop(2, near_pick)
    near_copies = []
    for i, q in enumerate(NEAR_ORDER):
        own = 8 - q
        near_copies.append(
            pltpu.make_async_remote_copy(
                src_ref=near_out.at[pl.ds((own - own // 5) * NCAP, NCAP)],
                dst_ref=near_in.at[pl.ds(i * NCAP, NCAP)],
                send_sem=near_send.at[i],
                recv_sem=near_recv.at[i],
                device_id=neighbour(own // 3 - 1, own % 3 - 1),
                device_id_type=MESH,
            )
        )
    for copy in near_copies:
        copy.start()

    def far_group(g):
        first = max(g * slots, 1)
        span = pl.ds(first * FAR, ((g + 1) * slots - first) * FAR)
        return pltpu.make_async_remote_copy(
            src_ref=far_out.at[span],
            dst_ref=far_in.at[span],
            send_sem=far_send.at[g],
            recv_sem=far_recv.at[g],
            device_id=device(lax.rem(me + 1, DEVICES)),
            device_id_type=MESH,
        )

    l_wp.wait()
    l_pe.wait()

    def process_first(step):
        here = rows(step, P_STEP)
        pos, row = columns(P_POS, step, P_STEP), columns(P_ROW, step, P_STEP)
        target = dot(onehot(row, 0, NODES), mid[...]).astype(BF16)
        pre[here, :] = dot(pe[here, :], weight(wp, 0)) + dot(target, weight(wp, 2))
        src[here, :] = dot(onehot(pos, 0, NODES), mid[...]).astype(BF16)

    loop(P_EDGES // P_STEP, process_first)
    l_wr.wait()

    def grid_step(step):
        here = rows(step, C_STEP)
        own = grid[here, :]
        hidden = silu(dot(own, weight(wr, 0)))
        branch = norm(dot(hidden, weight(wr, 1)), 2)
        updated = (own.astype(F32) + branch).astype(BF16)
        lines = C_STEP // grid_out.shape[1]
        grid_out[pl.ds(step * lines, lines)] = updated.reshape(lines, *grid_out.shape[1:])

    loop(GRID // C_STEP, grid_step)
    l_wn.wait()

    def out_first(step):
        here = rows(step, N_STEP)
        node_pre[here, :] = dot(mid[here, :], weight(wn, 0))

    loop(NODES // N_STEP, out_first)
    total[...] = jnp.zeros((NODES, D), F32)

    far_base = NODES + NEAR_ROWS
    last_base = NODES + NEAR_ROWS - LAST

    def last_spots(step):
        here = rows(step, P_STEP)
        last_hot[here, :] = onehot(columns(P_POS, step, P_STEP), last_base, LAST)
        sum_hot[:, pl.ds(pl.multiple_of(step * P_STEP, P_STEP), P_STEP)] = onehot_rows(
            P_ROW, step, P_STEP
        )

    loop(P_EDGES // P_STEP, last_spots)

    def take(count, base, arrived):
        def step_of(step):
            here = rows(step, P_STEP)
            off = columns(P_POS, step, P_STEP)
            src[here, :] += dot(onehot(off, base, count), arrived[...]).astype(BF16)

        loop(P_EDGES // P_STEP, step_of)

    def near_part(group):
        first, last = group
        for copy in near_copies[first:last]:
            copy.wait()
        return pl.ds(first * NCAP, (last - first) * NCAP)

    for g in range(FAR_GROUPS):
        far_group(g).wait()
        first = g * slots * FAR
        take(slots * FAR, far_base + first, far_in.at[pl.ds(first, slots * FAR)])
    for group in NEAR_GROUPS[:-1]:
        part = near_part(group)
        take(part.size, NODES + part.start, near_in.at[part])

    def project(step):
        here = rows(step, P_STEP)
        pre[here, :] += dot(src[here, :], weight(wp, 1))

    loop(P_EDGES // P_STEP, project)
    last = near_part(NEAR_GROUPS[-1])
    table[pl.ds(0, LAST), :] = dot(near_in[last, :], weight(wp, 1)).astype(BF16)

    def process_last(step):
        here = rows(step, P_STEP)
        hidden = silu(pre[here, :] + dot(last_hot[here, :], table[pl.ds(0, LAST), :]))
        branch = norm(dot(hidden, weight(wp, 3)), 3)
        updated = (pe[here, :].astype(F32) + branch).astype(BF16)
        hot = sum_hot[:, pl.ds(pl.multiple_of(step * P_STEP, P_STEP), P_STEP)]
        total[...] += dot(hot, updated)

    loop(P_EDGES // P_STEP, process_last)

    def out_last(step):
        here = rows(step, N_STEP)
        summed = total[here, :].astype(BF16)
        hidden = silu(node_pre[here, :] + dot(summed, weight(wn, 1)))
        branch = norm(dot(hidden, weight(wn, 2)), 4)
        mesh_out[here, :] = (mid[here, :].astype(F32) + branch).astype(BF16)

    loop(NODES // N_STEP, out_last)


def body(
    grid_nodes, mesh_nodes, g2m_edges, mesh_edges, g2m_sender, g2m_receiver, g2m_window,
    mesh_sender, mesh_receiver, mesh_window, near_rows, far_rows,
    w_g2m_edge, w_mesh_node, w_grid_node, w_proc_edge, w_proc_node, norms,
):
    smem = pl.BlockSpec(memory_space=pltpu.SMEM)
    any_space = pl.BlockSpec(memory_space=pl.ANY)

    def buf(count, dtype=BF16):
        return pltpu.VMEM((count, D), dtype)

    def ints(*shape):
        return pltpu.VMEM(shape, jnp.int32)

    dma = pltpu.SemaphoreType.DMA
    mesh_out, grid_out = pl.pallas_call(
        kernel,
        out_shape=(
            pltpu.VMEM((NODES, D), BF16),
            pltpu.VMEM(grid_nodes.shape, BF16),
        ),
        in_specs=[smem, smem] + [any_space] * 16,
        out_specs=(pl.BlockSpec(memory_space=pltpu.VMEM), pl.BlockSpec(memory_space=pltpu.VMEM)),
        scratch_shapes=[
            ints(G_BLOCKS, 128), ints(G_BLOCKS, 128), ints(P_BLOCKS, 128), ints(P_BLOCKS, 128),
            ints(9, 1, NCAP), ints(1, FAR, DEVICES), pltpu.VMEM((5, 2, D), F32), ints(64, 128),
            buf(GRID), buf(HALO_PAD), buf(128), buf(NODES), buf(G_EDGES), buf(P_EDGES),
            buf(4 * D), buf(3 * D), buf(2 * D), buf(4 * D), buf(3 * D),
            buf(P_EDGES, F32), buf(P_EDGES), buf(NODES, F32), buf(NODES, F32), buf(NODES),
            buf(NEAR_ROWS), buf(NEAR_ROWS), buf(DEVICES * FAR), buf(DEVICES * FAR),
            buf(DEVICES * FAR), buf(HALO_PAD), buf(GRID),
            pltpu.VMEM((P_EDGES, LAST), BF16), pltpu.VMEM((NODES, P_EDGES), BF16),
            dma((16,)), dma((8,)), dma((8,)), dma((8,)), dma((8,)),
            dma((FAR_GROUPS,)), dma((FAR_GROUPS,)), pltpu.SemaphoreType.REGULAR,
        ],
        compiler_params=pltpu.CompilerParams(
            collective_id=0, has_side_effects=True, vmem_limit_bytes=60 * 2**20
        ),
    )(
        g2m_window, mesh_window,
        g2m_sender, g2m_receiver, mesh_sender, mesh_receiver, near_rows.transpose(1, 0, 2), far_rows.transpose(0, 2, 1), norms,
        grid_nodes.reshape(GRID, D), mesh_nodes, g2m_edges.reshape(-1, D), mesh_edges.reshape(-1, D),
        w_g2m_edge.reshape(-1, D), w_mesh_node.reshape(-1, D), w_grid_node.reshape(-1, D),
        w_proc_edge.reshape(-1, D), w_proc_node.reshape(-1, D),
    )
    return mesh_out, grid_out


def solution(mesh):
    both = ("lat", "lon")
    return jax.shard_map(
        body,
        mesh=mesh,
        in_specs=(
            P("lat", "lon", None), P(both, None), P(both, None, None), P(both, None, None),
            P(both, None), P(both, None), P(both), P(both, None), P(both, None), P(both),
            P(both, None, None), P(both, None, None),
            P(), P(), P(), P(), P(), P(),
        ),
        out_specs=(P(both, None), P("lat", "lon", None)),
        check_vma=False,
    )
```

```python
import jax
import jax.numpy as jnp
from jax import lax
from jax.experimental import pallas as pl
from jax.experimental.pallas import tpu as pltpu
from jax.sharding import PartitionSpec as P

HW = 4
EPS = 1e-05
D = 512
BF16 = jnp.bfloat16
F32 = jnp.float32
MESH = pl.DeviceIdType.MESH

GRID = 1024
HALO = 704
HALO_PAD = 768
NODES = 512
NCAP = 192
NEAR = 9 * NCAP
NEAR_ORDER = (1, 7, 3, 5, 0, 2, 6, 8)
NEAR_ROWS = 8 * NCAP
NEAR_GROUPS = ((0, 2), (2, 4), (4, 8))
LAST = (NEAR_GROUPS[-1][1] - NEAR_GROUPS[-1][0]) * NCAP
FAR = 16
DEVICES = 128
G_EDGES = 1792
P_EDGES = 2048
E_STEP = 1792
P_STEP = 2048
N_STEP = 512
C_STEP = 512
F_STEP = 1024

G_POS, G_ROW, P_POS, P_ROW = 0, 16, 32, 48
G_BLOCKS, P_BLOCKS = 14, 16

FAR_MUL = 77
FAR_INV = 5
FAR_GROUPS = 2
HOP = 12
HOPS = 10

SEGMENTS = (
    (0, 1, 512, 64),
    (0, -1, 576, 64),
    (1, 1, 640, 16),
    (1, -1, 656, 16),
    (-1, 1, 672, 16),
    (-1, -1, 688, 16),
    (1, 0, 0, 256),
    (-1, 0, 256, 256),
)


def dot(a, b):
    return jnp.dot(a, b, preferred_element_type=F32)


def silu(v):
    half = 0.5 * v
    return (half + half * jnp.tanh(half)).astype(BF16)


def layer_norm(values, gain, shift):
    mean = jnp.mean(values, axis=-1, keepdims=True)
    centred = values - mean
    variance = jnp.mean(centred * centred, axis=-1, keepdims=True)
    return centred * lax.rsqrt(variance + EPS) * gain + shift


def grid_spots(sender):
    i = (sender * 14564) >> 20
    j = sender - 72 * i
    north, south = i < HW, i >= 20
    west, east = j < HW, j >= 68
    edge, side = north | south, west | east
    band = jnp.where(north, i, jnp.where(south, i - 20, i - HW))
    sector = jnp.where(west, j, jnp.where(east, j - 68, j - HW))
    corner = 1664 + jnp.where(south, 32, 0) + jnp.where(east, 16, 0)
    base = jnp.where(
        edge,
        jnp.where(side, corner, jnp.where(north, 1024, 1280)),
        jnp.where(west, 1536, jnp.where(east, 1600, 0)),
    )
    return base + band * jnp.where(side, 4, 64) + sector


def source_spots(sender, me):
    far = sender - (NODES + NEAR)
    place = (((me - (far >> 4)) & (DEVICES - 1)) * FAR_INV) & (DEVICES - 1)
    near = sender - NODES
    q = (near * 10923) >> 21
    order = jnp.zeros_like(q)
    for i, position in enumerate(NEAR_ORDER):
        order = jnp.where(q == position, i, order)
    near_spot = NODES + order * NCAP + near - q * NCAP
    far_spot = NODES + NEAR_ROWS + place * FAR + (far & (FAR - 1))
    return jnp.where(far >= 0, far_spot, jnp.where(near >= 0, near_spot, sender))


def kernel(
    g_window, p_window,
    gs_h, gr_h, ps_h, pr_h, near_h, far_h, norms_h,
    grid_h, mesh_h, ge_h, pe_h, wg_h, wm_h, wr_h, wp_h, wn_h,
    mesh_out, grid_out,
    gs, gr, ps, pr, near, far, norms, idx,
    grid, halo, strips, mesh, ge, pe, wg, wm, wr, wp, wn,
    pre, src, total, node_pre, mid, near_out, near_in, far_out, far_in,
    far_hot, table, cells, last_hot, sum_hot,
    load_sem, halo_send, halo_recv, near_send, near_recv, far_send, far_recv, round_sem,
):
    lat, lon = lax.axis_index("lat"), lax.axis_index("lon")
    me = lat * 16 + lon

    def device(p):
        return (lax.div(p, 16), lax.rem(p, 16))

    def neighbour(band, sector):
        return (lax.rem(lat + band + 8, 8), lax.rem(lon + sector + 16, 16))

    loads = [
        pltpu.make_async_copy(h, v, load_sem.at[i])
        for i, (h, v) in enumerate(
            ((grid_h, grid), (gs_h, gs), (gr_h, gr), (mesh_h, mesh), (ge_h, ge), (wg_h, wg),
             (ps_h, ps), (pr_h, pr), (near_h, near), (far_h, far), (norms_h, norms), (wm_h, wm),
             (wp_h, wp), (pe_h, pe), (wr_h, wr), (wn_h, wn))
        )
    ]
    for copy in loads:
        copy.start()
    l_grid, l_gs, l_gr, l_mesh, l_ge, l_wg = loads[:6]
    l_small, (l_wm, l_wp, l_pe, l_wr, l_wn) = loads[6:11], loads[11:]

    halo[pl.ds(HALO, HALO_PAD - HALO), :] = jnp.zeros((HALO_PAD - HALO, D), BF16)
    far_in[pl.ds(0, FAR), :] = jnp.zeros((FAR, D), BF16)

    barrier = pltpu.get_barrier_semaphore()

    def greet(to):
        pl.semaphore_signal(barrier, inc=1, device_id=to, device_id_type=MESH)

    for band, sector, _, _ in SEGMENTS:
        greet(neighbour(band, sector))
    steps_back = [HOP * j for j in range(1, HOPS + 1)] + list(range(1, HOP))
    for back in steps_back:
        greet(device(lax.rem(me + DEVICES - back, DEVICES)))

    lane = lax.broadcasted_iota(jnp.int32, (128, 128), 1)

    def offsets(first, b):
        row = idx[pl.ds(first + b, 1), :]
        return jnp.broadcast_to(row, (128, 128)).T - lane

    def columns(first, step, count):
        blocks = count // 128
        return jnp.concatenate([offsets(first, step * blocks + b) for b in range(blocks)], axis=0)

    def node_rows(receiver, window, first, count):
        for b in range(count):
            row = receiver[pl.ds(b, 1), :]
            idx[pl.ds(first + b, 1), :] = jnp.where(row >= 0, row + 128 * window[b], -1)

    def onehot(off, base, count):
        return jnp.concatenate(
            [jnp.where(off == base + 128 * k, 1.0, 0.0).astype(BF16) for k in range(count // 128)],
            axis=1,
        )

    def onehot_rows(first, step, count):
        blocks = count // 128
        row = jnp.concatenate(
            [idx[pl.ds(first + step * blocks + b, 1), :] for b in range(blocks)], axis=1
        )
        node = lax.broadcasted_iota(jnp.int32, (NODES, count), 0)
        return jnp.where(node == row, 1.0, 0.0).astype(BF16)

    def rows(step, count):
        return pl.ds(pl.multiple_of(step * count, count), count)

    def weight(ref, i):
        return ref[pl.ds(i * D, D), :]

    def norm(values, i):
        return layer_norm(values, norms[i, pl.ds(0, 1), :], norms[i, pl.ds(1, 1), :])

    def loop(count, body):
        def run(step, carry):
            body(step)
            return carry

        lax.fori_loop(0, count, run, 0)

    l_grid.wait()
    spot = lax.broadcasted_iota(jnp.int32, (128, GRID), 0)
    cell = lax.broadcasted_iota(jnp.int32, (128, GRID), 1)
    wanted = jnp.where(spot < 64, 0, 60 - 1024) + lax.div(spot, 4) * 64 + lax.rem(spot, 4)
    strips[...] = dot(jnp.where(cell == wanted, 1.0, 0.0).astype(BF16), grid[...]).astype(BF16)

    sources = (
        strips.at[pl.ds(64, 64)], strips.at[pl.ds(0, 64)],
        strips.at[pl.ds(112, 16)], strips.at[pl.ds(48, 16)],
        strips.at[pl.ds(64, 16)], strips.at[pl.ds(0, 16)],
        grid.at[pl.ds(768, 256)], grid.at[pl.ds(0, 256)],
    )
    pl.semaphore_wait(barrier, len(SEGMENTS) + len(steps_back))
    halo_copies = [
        pltpu.make_async_remote_copy(
            src_ref=source,
            dst_ref=halo.at[pl.ds(first, count)],
            send_sem=halo_send.at[i],
            recv_sem=halo_recv.at[i],
            device_id=neighbour(band, sector),
            device_id_type=MESH,
        )
        for i, ((band, sector, first, count), source) in enumerate(zip(SEGMENTS, sources))
    ]
    for copy in halo_copies:
        copy.start()
    for ahead in range(1, HOP):
        pl.semaphore_signal(
            round_sem, inc=1, device_id=device(lax.rem(me + ahead, DEVICES)), device_id_type=MESH
        )

    l_gs.wait()
    l_gr.wait()
    idx[pl.ds(G_POS, G_BLOCKS), :] = grid_spots(gs[...])
    node_rows(gr, g_window, G_ROW, G_BLOCKS)
    l_ge.wait()
    l_mesh.wait()
    l_wg.wait()

    table[pl.ds(0, NODES), :] = dot(mesh[...], weight(wg, 2)).astype(BF16)
    cells[...] = dot(grid[...], weight(wg, 1)).astype(BF16)

    def encode_first(step):
        here = rows(step, E_STEP)
        row = columns(G_ROW, step, E_STEP)
        pos = columns(G_POS, step, E_STEP)
        pre[here, :] = (
            dot(ge[here, :], weight(wg, 0))
            + dot(onehot(row, 0, NODES), table[pl.ds(0, NODES), :])
            + dot(onehot(pos, 0, GRID), cells[...])
        )

    loop(G_EDGES // E_STEP, encode_first)
    for copy in l_small:
        copy.wait()
    idx[pl.ds(P_POS, P_BLOCKS), :] = source_spots(ps[...], me)
    node_rows(pr, p_window, P_ROW, P_BLOCKS)

    edge = lax.broadcasted_iota(jnp.int32, (F_STEP, DEVICES), 0)
    lane_of = lax.broadcasted_iota(jnp.int32, (F_STEP, DEVICES), 1)
    part = lax.broadcasted_iota(jnp.int32, (F_STEP, 2 * FAR), 1)
    of_slot = (
        (lax.broadcasted_iota(jnp.int32, (F_STEP, 2 * FAR), 0) & (FAR - 1)) == (part & (FAR - 1))
    )
    spread = jnp.where(
        lax.broadcasted_iota(jnp.int32, (2 * FAR, 128), 0) < FAR, 16.0, 1.0
    ).astype(BF16)
    lists = jnp.concatenate([far[0] >> 4, far[0] & 15], axis=0).astype(F32).astype(BF16)

    def far_spots(step):
        place = (edge >> 4) + step * (F_STEP // FAR)
        of_list = jnp.where(((me + place * FAR_MUL) & (DEVICES - 1)) == lane_of, 1.0, 0.0).astype(BF16)
        mine = lax.dot_general(
            of_list, lists, (((1,), (1,)), ((), ())), preferred_element_type=F32
        )
        node = dot(jnp.where(of_slot, mine, 0.0).astype(BF16), spread)
        off = node - lane_of.astype(F32)
        far_hot[rows(step, F_STEP), :] = jnp.concatenate(
            [jnp.where(off == 128.0 * k, 1.0, 0.0).astype(BF16) for k in range(NODES // 128)], axis=1
        )

    loop(DEVICES * FAR // F_STEP, far_spots)
    l_wm.wait()

    def node_first(step):
        here = rows(step, N_STEP)
        node_pre[here, :] = dot(mesh[here, :], weight(wm, 0))

    loop(NODES // N_STEP, node_first)
    for copy in halo_copies:
        copy.wait()

    table[pl.ds(0, HALO_PAD), :] = dot(halo[...], weight(wg, 1)).astype(BF16)

    def encode_last(step):
        here = rows(step, E_STEP)
        pos = columns(G_POS, step, E_STEP)
        hidden = silu(pre[here, :] + dot(onehot(pos, GRID, HALO_PAD), table[pl.ds(0, HALO_PAD), :]))
        branch = norm(dot(hidden, weight(wg, 3)), 0)
        updated = (ge[here, :].astype(F32) + branch).astype(BF16)
        total[...] = dot(onehot_rows(G_ROW, step, E_STEP), updated)

    encode_last(0)

    def node_last(step):
        here = rows(step, N_STEP)
        summed = total[here, :].astype(BF16)
        hidden = silu(node_pre[here, :] + dot(summed, weight(wm, 1)))
        branch = norm(dot(hidden, weight(wm, 2)), 1)
        mid[here, :] = (mesh[here, :].astype(F32) + branch).astype(BF16)

    loop(NODES // N_STEP, node_last)

    def far_pick(step):
        here = rows(step, F_STEP)
        far_out[here, :] = dot(far_hot[here, :], mid[...]).astype(BF16)

    slots = DEVICES // FAR_GROUPS

    def far_copy(k, g):
        there = pl.ds(pl.multiple_of(k * FAR, FAR), FAR)
        return pltpu.make_async_remote_copy(
            src_ref=far_out.at[there],
            dst_ref=far_in.at[there],
            send_sem=far_send.at[g],
            recv_sem=far_recv.at[g],
            device_id=device(lax.rem(me + k * FAR_MUL, DEVICES)),
            device_id_type=MESH,
        )

    for g in range(FAR_GROUPS):
        far_pick(g)
        if g == 0:
            pl.semaphore_wait(round_sem, HOP - 1)

        def send(k, carry, g=g):
            far_copy(k, g).start()
            return carry

        lax.fori_loop(max(g * slots, 1), (g + 1) * slots, send, 0)

    def near_columns(q):
        row = near[q]
        first = jnp.broadcast_to(row[:, :128], (128, 128)).T - lane
        second = jnp.broadcast_to(row[:, 64:], (128, 128)).T - lane
        return jnp.concatenate([first, second[64:]], axis=0)

    def near_pick(half):
        off = jnp.concatenate([near_columns(5 * half + i) for i in range(4)], axis=0)
        picked = dot(onehot(off, 0, NODES), mid[...]).astype(BF16)
        near_out[pl.ds(pl.multiple_of(half * 4 * NCAP, 4 * NCAP), 4 * NCAP), :] = picked

    loop(2, near_pick)
    near_copies = []
    for i, q in enumerate(NEAR_ORDER):
        own = 8 - q
        near_copies.append(
            pltpu.make_async_remote_copy(
                src_ref=near_out.at[pl.ds((own - own // 5) * NCAP, NCAP)],
                dst_ref=near_in.at[pl.ds(i * NCAP, NCAP)],
                send_sem=near_send.at[i],
                recv_sem=near_recv.at[i],
                device_id=neighbour(own // 3 - 1, own % 3 - 1),
                device_id_type=MESH,
            )
        )
    for copy in near_copies:
        copy.start()

    def far_group(g):
        first = max(g * slots, 1)
        span = pl.ds(first * FAR, ((g + 1) * slots - first) * FAR)
        return pltpu.make_async_remote_copy(
            src_ref=far_out.at[span],
            dst_ref=far_in.at[span],
            send_sem=far_send.at[g],
            recv_sem=far_recv.at[g],
            device_id=device(lax.rem(me + 1, DEVICES)),
            device_id_type=MESH,
        )

    l_wp.wait()
    l_pe.wait()

    def process_first(step):
        here = rows(step, P_STEP)
        pos, row = columns(P_POS, step, P_STEP), columns(P_ROW, step, P_STEP)
        target = dot(onehot(row, 0, NODES), mid[...]).astype(BF16)
        pre[here, :] = dot(pe[here, :], weight(wp, 0)) + dot(target, weight(wp, 2))
        src[here, :] = dot(onehot(pos, 0, NODES), mid[...]).astype(BF16)

    loop(P_EDGES // P_STEP, process_first)
    l_wr.wait()

    def grid_step(step):
        here = rows(step, C_STEP)
        own = grid[here, :]
        hidden = silu(dot(own, weight(wr, 0)))
        branch = norm(dot(hidden, weight(wr, 1)), 2)
        updated = (own.astype(F32) + branch).astype(BF16)
        lines = C_STEP // grid_out.shape[1]
        grid_out[pl.ds(step * lines, lines)] = updated.reshape(lines, *grid_out.shape[1:])

    loop(GRID // C_STEP, grid_step)
    l_wn.wait()

    def out_first(step):
        here = rows(step, N_STEP)
        node_pre[here, :] = dot(mid[here, :], weight(wn, 0))

    loop(NODES // N_STEP, out_first)

    far_base = NODES + NEAR_ROWS
    last_base = NODES + NEAR_ROWS - LAST

    def last_spots(step):
        here = rows(step, P_STEP)
        last_hot[here, :] = onehot(columns(P_POS, step, P_STEP), last_base, LAST)
        sum_hot[:, pl.ds(pl.multiple_of(step * P_STEP, P_STEP), P_STEP)] = onehot_rows(
            P_ROW, step, P_STEP
        )

    loop(P_EDGES // P_STEP, last_spots)

    def take(count, base, arrived):
        def step_of(step):
            here = rows(step, P_STEP)
            off = columns(P_POS, step, P_STEP)
            src[here, :] += dot(onehot(off, base, count), arrived[...]).astype(BF16)

        loop(P_EDGES // P_STEP, step_of)

    def near_part(group):
        first, last = group
        for copy in near_copies[first:last]:
            copy.wait()
        return pl.ds(first * NCAP, (last - first) * NCAP)

    for g in range(FAR_GROUPS):
        far_group(g).wait()
        first = g * slots * FAR
        take(slots * FAR, far_base + first, far_in.at[pl.ds(first, slots * FAR)])
    for group in NEAR_GROUPS[:-1]:
        part = near_part(group)
        take(part.size, NODES + part.start, near_in.at[part])

    def project(step):
        here = rows(step, P_STEP)
        pre[here, :] += dot(src[here, :], weight(wp, 1))

    loop(P_EDGES // P_STEP, project)
    last = near_part(NEAR_GROUPS[-1])
    table[pl.ds(0, LAST), :] = dot(near_in[last, :], weight(wp, 1)).astype(BF16)

    def process_last(step):
        here = rows(step, P_STEP)
        hidden = silu(pre[here, :] + dot(last_hot[here, :], table[pl.ds(0, LAST), :]))
        branch = norm(dot(hidden, weight(wp, 3)), 3)
        updated = (pe[here, :].astype(F32) + branch).astype(BF16)
        hot = sum_hot[:, pl.ds(pl.multiple_of(step * P_STEP, P_STEP), P_STEP)]
        total[...] = dot(hot, updated)

    process_last(0)

    def out_last(step):
        here = rows(step, N_STEP)
        summed = total[here, :].astype(BF16)
        hidden = silu(node_pre[here, :] + dot(summed, weight(wn, 1)))
        branch = norm(dot(hidden, weight(wn, 2)), 4)
        mesh_out[here, :] = (mid[here, :].astype(F32) + branch).astype(BF16)

    loop(NODES // N_STEP, out_last)


def body(
    grid_nodes, mesh_nodes, g2m_edges, mesh_edges, g2m_sender, g2m_receiver, g2m_window,
    mesh_sender, mesh_receiver, mesh_window, near_rows, far_rows,
    w_g2m_edge, w_mesh_node, w_grid_node, w_proc_edge, w_proc_node, norms,
):
    smem = pl.BlockSpec(memory_space=pltpu.SMEM)
    any_space = pl.BlockSpec(memory_space=pl.ANY)

    def buf(count, dtype=BF16):
        return pltpu.VMEM((count, D), dtype)

    def ints(*shape):
        return pltpu.VMEM(shape, jnp.int32)

    dma = pltpu.SemaphoreType.DMA
    mesh_out, grid_out = pl.pallas_call(
        kernel,
        out_shape=(
            pltpu.VMEM((NODES, D), BF16),
            pltpu.VMEM(grid_nodes.shape, BF16),
        ),
        in_specs=[smem, smem] + [any_space] * 16,
        out_specs=(pl.BlockSpec(memory_space=pltpu.VMEM), pl.BlockSpec(memory_space=pltpu.VMEM)),
        scratch_shapes=[
            ints(G_BLOCKS, 128), ints(G_BLOCKS, 128), ints(P_BLOCKS, 128), ints(P_BLOCKS, 128),
            ints(9, 1, NCAP), ints(1, FAR, DEVICES), pltpu.VMEM((5, 2, D), F32), ints(64, 128),
            buf(GRID), buf(HALO_PAD), buf(128), buf(NODES), buf(G_EDGES), buf(P_EDGES),
            buf(4 * D), buf(3 * D), buf(2 * D), buf(4 * D), buf(3 * D),
            buf(P_EDGES, F32), buf(P_EDGES), buf(NODES, F32), buf(NODES, F32), buf(NODES),
            buf(NEAR_ROWS), buf(NEAR_ROWS), buf(DEVICES * FAR), buf(DEVICES * FAR),
            buf(DEVICES * FAR), buf(HALO_PAD), buf(GRID),
            pltpu.VMEM((P_EDGES, LAST), BF16), pltpu.VMEM((NODES, P_EDGES), BF16),
            dma((16,)), dma((8,)), dma((8,)), dma((8,)), dma((8,)),
            dma((FAR_GROUPS,)), dma((FAR_GROUPS,)), pltpu.SemaphoreType.REGULAR,
        ],
        compiler_params=pltpu.CompilerParams(
            collective_id=0, has_side_effects=True, vmem_limit_bytes=60 * 2**20
        ),
    )(
        g2m_window, mesh_window,
        g2m_sender, g2m_receiver, mesh_sender, mesh_receiver, near_rows.transpose(1, 0, 2), far_rows.transpose(0, 2, 1), norms,
        grid_nodes.reshape(GRID, D), mesh_nodes, g2m_edges.reshape(-1, D), mesh_edges.reshape(-1, D),
        w_g2m_edge.reshape(-1, D), w_mesh_node.reshape(-1, D), w_grid_node.reshape(-1, D),
        w_proc_edge.reshape(-1, D), w_proc_node.reshape(-1, D),
    )
    return mesh_out, grid_out


def solution(mesh):
    both = ("lat", "lon")
    return jax.shard_map(
        body,
        mesh=mesh,
        in_specs=(
            P("lat", "lon", None), P(both, None), P(both, None, None), P(both, None, None),
            P(both, None), P(both, None), P(both), P(both, None), P(both, None), P(both),
            P(both, None, None), P(both, None, None),
            P(), P(), P(), P(), P(), P(),
        ),
        out_specs=(P(both, None), P("lat", "lon", None)),
        check_vma=False,
    )
```
